128 devices in a mesh: op: 32 (over z_lo, y, x), blk: 4 (over z_hi, core).
Axes of the slice: x: 4, y: 4, z: 4 (z_hi: 2, z_lo: 2; z = z_hi * 2 + z_lo), core: 2. Of those that a mesh axis runs over, the one named last changes fastest.
Arguments:
- wave_blocks: bfloat16 [16, 256, 256], P('blk'), may hold values from -6 to 6
- left_env: bfloat16 [512, 16, 256, 256], P('op', 'blk'), may hold values from -0.375 to 0.375
- right_env: bfloat16 [512, 16, 256, 256], P('op', 'blk'), may hold values from -0.015625 to 0.015625
- source: int32 [512, 16], P('op', 'blk'), may hold values from 0 to 15
- block_dims: int32 [2, 16], P(None, 'blk'), may hold values from 64 to 256, as said below
- energy: float32 [16], P('blk'), may hold values from 0.5 to 3
Outputs:
- applied_wave: float32 [16, 256, 256], P('blk')
- applied_corr: float32 [16, 256, 256], P('blk')
The draws below stay inside these ranges and needn't reach their ends.
Inputs may be any that keep to these rules, and one draw needn't show every extreme that they name: `source`: each entry names a block. `block_dims`: 256 is reached in every draw.
All inputs are finite; a program needn't handle non-finite values.
Results may differ from the reference program's by a relative error of at most 0.0037.
Values may be sent and summed in bfloat16 or wider, within the bound.
No kernel may reach another device: no remote copies, remote signals or barrier semaphores. Data moves between devices by JAX's collectives and lax.ppermute only.
A program may use at most 64 MiB of HBM per device.

```python
import jax
import jax.numpy as jnp
from jax import lax

BD = 256
BLK_DEV = 4
NBLK = 16
TERMS = 512
N_BLK = 4


def draw_block_dims(key, part):
    key = jax.random.fold_in(key, 5)
    dims_drawn = jax.random.randint(key, (2, NBLK), BD // 4, BD + 1)
    picked = jax.random.randint(jax.random.fold_in(key, 1), (2,), 0, NBLK)
    blocks_iota = jnp.arange(NBLK, dtype=jnp.int32)
    hit = blocks_iota[None, :] == picked[:, None]
    return jnp.where(hit, BD, dims_drawn).astype(jnp.int32)


def touch_ends(result, rng, least, largest):
    shape = result.shape
    index_at = [jax.random.randint(jax.random.fold_in(rng, axis), (), 0, shape[axis]) for axis in range(len(shape))]
    result = result.at[tuple(index_at)].set(least)
    longest = shape.index(max(shape))
    index_at[longest] = (index_at[longest] + 1) % shape[longest]
    return result.at[tuple(index_at)].set(largest)


def steps_of(stream_key, shape, split, least, top_value):
    level = 1.0
    for dim, parts in split:
        steps = jax.random.uniform(jax.random.fold_in(jax.random.fold_in(stream_key, 6), dim), (parts,), jnp.float32, least / len(split), top_value / len(split))
        level = level * jnp.repeat(jnp.exp(steps), shape[dim] // parts).reshape((-1,) + (1,) * (len(shape) - 1 - dim))
    return level


def gaussian(stream_key, extent, width, reach, shards=(), kind=jnp.bfloat16):
    result = jax.random.normal(stream_key, extent, jnp.float32) * width
    if len(shards) > 0:
        result = steps_of(stream_key, extent, shards, -0.22, 0.18) * result
    return jnp.clip(result, min=-reach, max=reach).astype(kind)


def setup_inputs(seed: int = 0) -> dict:
    streams_of = jax.random.split(jax.random.key(seed), 7)
    return {
        "wave_blocks": gaussian(streams_of[0], (NBLK, BD, BD), 1.0, 6.0, ((0, 4),)),
        "left_env": gaussian(streams_of[1], (TERMS, NBLK, BD, BD), BD ** -0.5, 0.375, ((0, 32), (1, 4))),
        "right_env": gaussian(streams_of[2], (TERMS, NBLK, BD, BD), (BD * TERMS) ** -0.5, 0.015625, ((0, 32), (1, 4))),
        "source": touch_ends(jax.random.randint(streams_of[3], (TERMS, NBLK), 0, NBLK), jax.random.fold_in(streams_of[3], 1), 0, NBLK - 1).astype(jnp.int32),
        "block_dims": draw_block_dims(jax.random.fold_in(streams_of[6], 71), 0),
        "energy": jnp.clip(0.5 + 2.5 * jax.random.uniform(streams_of[5], (NBLK,), jnp.float32) ** steps_of(streams_of[5], (NBLK,), ((0, 4),), -0.2, 0.2), 0.5, 3.0),
    }


def live_mask(block_dims, offset, row_count, block_size):
    row_ids = offset + jnp.arange(row_count, dtype=jnp.int32)
    col_ids = jnp.arange(block_size, dtype=jnp.int32)
    rows_ok = row_ids[None, :, None] < block_dims[0][:, None, None]
    cols_ok = col_ids[None, None, :] < block_dims[1][:, None, None]
    return rows_ok & cols_ok

def slot_order():
    blocks_iota = jnp.arange(NBLK, dtype=jnp.int32)
    digit_high = blocks_iota // BLK_DEV
    digit_mid = blocks_iota % BLK_DEV // N_BLK
    digit_low = blocks_iota % N_BLK
    return (digit_low * BLK_DEV + digit_mid * N_BLK + digit_high).astype(jnp.int32)

def apply_terms(vector, left_env, right_env, source):

    def add_term(total, pieces):
        left_term, right_term, source_term = pieces
        chosen = jnp.take(vector, source_term, axis=0).astype(jnp.float32)
        inner = jnp.einsum('eij,ejk->eik', left_term.astype(jnp.float32), chosen).astype(jnp.bfloat16)
        inner = lax.optimization_barrier(inner)
        return (total + jnp.einsum('eik,elk->eil', inner.astype(jnp.float32), right_term.astype(jnp.float32)), None)
    zeros = jnp.zeros((NBLK, BD, BD), jnp.float32)
    total, unused = lax.scan(add_term, zeros, (left_env, right_env, source))
    return total

def reference(wave_blocks, left_env, right_env, source, block_dims, energy):
    live = live_mask(block_dims, 0, BD, BD)
    wave_live = jnp.where(live, wave_blocks, jnp.zeros_like(wave_blocks))
    slots = slot_order()

    def apply_hamiltonian(vector):
        total = apply_terms(vector, left_env, right_env, source)
        summed = jnp.take(total, slots, axis=0) + energy[:, None, None] * vector.astype(jnp.float32)
        return jnp.where(live, summed, jnp.zeros_like(summed))
    applied_wave = apply_hamiltonian(wave_live)
    entries = NBLK * BD * BD
    wave_float = wave_live.astype(jnp.float32)
    rayleigh = jnp.sum(wave_float * applied_wave) / entries / (jnp.sum(wave_float * wave_float) / entries + 1e-06)
    residual = applied_wave - rayleigh * wave_float
    correction = (residual * lax.rsqrt(jnp.sum(residual * residual) / entries + 1e-06)).astype(jnp.bfloat16)
    applied_corr = apply_hamiltonian(correction)
    return (applied_wave, applied_corr)
```

```python
import functools

import jax
import jax.numpy as jnp
from jax import lax
from jax.experimental import pallas as pl
from jax.experimental.pallas import tpu as pltpu
from jax.sharding import PartitionSpec as P

BF = jnp.bfloat16
F32 = jnp.float32
BD = 256
INFO = 32
ROWS = 4 * BD + INFO
STEP = 2
MIB = 1 << 20
ALL = ("op", "blk")

SMEM = pl.BlockSpec(memory_space=pltpu.SMEM)
VMEM = pl.BlockSpec(memory_space=pltpu.VMEM)


def device(op, blk):
    return op * 4 + blk


def cross_pairs():
    return [(device(o, b), device(o ^ 16, b ^ 2)) for o in range(32) for b in range(4)]


def core_pairs():
    return [(b, b ^ 1) for b in range(4)]


def core_groups():
    return [[device(o, zh * 2 + c) for zh in range(2) for o in range(32)] for c in range(2)]


def live(rows, cols, shape):
    row_ids = lax.broadcasted_iota(jnp.int32, shape, 0).astype(F32)
    col_ids = lax.broadcasted_iota(jnp.int32, shape, 1).astype(F32)
    return (row_ids < rows) & (col_ids < cols)


def pack_kernel(dims, energy, wave, out):
    for b in range(4):
        mask = live(dims[0, b].astype(F32), dims[1, b].astype(F32), (BD, BD))
        block = jnp.where(mask, wave[b].astype(F32), 0.0)
        out[b * BD:(b + 1) * BD, :] = block.astype(BF)
    row = lax.broadcasted_iota(jnp.int32, (INFO, BD), 0)
    info = jnp.zeros((INFO, BD), F32)
    for b in range(4):
        value = jnp.full((INFO, BD), energy[b], F32)
        high = value.astype(BF).astype(F32)
        middle = (value - high).astype(BF).astype(F32)
        low = value - high - middle
        parts = (dims[0, b].astype(F32), dims[1, b].astype(F32), high, middle, low)
        for j, part in enumerate(parts):
            info = jnp.where(row == b * 8 + j, part, info)
    out[4 * BD:, :] = info.astype(BF)


def add_terms(step, src, vec, left, right, acc):
    for e in range(4):
        total = None
        for t in range(STEP):
            chosen = vec[src[step * STEP + t, e]]
            inner = jnp.dot(left[t, e], chosen, preferred_element_type=F32).astype(BF)
            term = lax.dot_general(
                inner, right[t, e], (((1,), (1,)), ((), ())), preferred_element_type=F32
            )
            total = term if total is None else total + term
        acc[e] += total


def wave_kernel(src, ids, own, far, core, far_core, left, right, out, vec, acc):
    step = pl.program_id(0)

    @pl.when(step == 0)
    def _():
        acc[...] = jnp.zeros_like(acc)
        for flip, piece in ((0, own), (2, far), (1, core), (3, far_core)):
            group = ids[0] ^ flip
            for b in range(4):
                vec[group * 4 + b] = piece[b * BD:(b + 1) * BD, :]

    add_terms(step, src, vec, left, right, acc)

    @pl.when(step == pl.num_programs(0) - 1)
    def _():
        out[...] = acc[...].astype(BF)


def fold(x):
    return jnp.sum(x.reshape(BD // 8, 8, BD), axis=0)


def total_of(x):
    return jnp.sum(jnp.sum(x, axis=1, keepdims=True), axis=0, keepdims=True)


def corr_kernel(
    src, ids, own, far, core, far_core, same, other, left, right,
    applied_out, corr_out, out, vec, acc, work,
):
    step = pl.program_id(0)
    entries = 16 * BD * BD

    @pl.when(step == 0)
    def _():
        me = ids[0]
        pieces = ((0, own), (2, far), (1, core), (3, far_core))
        cross = jnp.zeros((8, BD), F32)
        square = jnp.zeros((8, BD), F32)
        for flip, piece in pieces:
            group = me ^ flip
            for turn in range(4):
                b = me ^ turn
                summed = (same if turn % 2 == 0 else other)[b >> 1, group].astype(F32)
                info = piece[4 * BD:, :].astype(F32)
                pick = lax.broadcasted_iota(jnp.int32, (INFO, BD), 0)

                def entry(j):
                    return jnp.sum(jnp.where(pick == b * 8 + j, info, 0.0), axis=0, keepdims=True)

                mask = live(entry(0), entry(1), (BD, BD))
                level = entry(2) + entry(3) + entry(4)
                wave = piece[pl.ds(pl.multiple_of(b * BD, BD), BD), :].astype(F32)
                applied = jnp.where(mask, summed, 0.0) + level * wave
                work[group * 4 + b] = applied
                if flip == 0:
                    applied_out[b] = applied
                cross += fold(applied * wave)
                square += fold(wave * wave)
        rayleigh = total_of(cross) / entries / (total_of(square) / entries + 1e-06)
        resid = jnp.zeros((8, BD), F32)
        for flip, piece in pieces:
            group = me ^ flip
            for b in range(4):
                wave = piece[b * BD:(b + 1) * BD, :].astype(F32)
                left_over = work[group * 4 + b] - rayleigh * wave
                work[group * 4 + b] = left_over
                resid += fold(left_over * left_over)
        scale = lax.rsqrt(total_of(resid) / entries + 1e-06)
        for b in range(16):
            vec[b] = (work[b] * scale).astype(BF)
        for b in range(4):
            corr_out[b] = vec[me * 4 + b]
        acc[...] = jnp.zeros_like(acc)

    add_terms(step, src, vec, left, right, acc)

    @pl.when(step == pl.num_programs(0) - 1)
    def _():
        for e in range(4):
            for i in range(16):
                for j in range(2):
                    tile = acc[e, i * 16:(i + 1) * 16, j * 128:(j + 1) * 128]
                    out[i * 2 + j, e] = tile.astype(BF)


def reduce_kernel(parts, out):
    total = jnp.sum(parts[...].astype(F32), axis=0).astype(BF)
    for i in range(out.shape[0]):
        out[i] = total


def reduce_blocks_kernel(parts, out):
    total = jnp.sum(parts[...].astype(F32), axis=0).astype(BF)
    for i in range(out.shape[0]):
        out[i] = total


def final_kernel(dims, energy, parts, corr, out):
    for b in range(4):
        mask = live(dims[0, b].astype(F32), dims[1, b].astype(F32), (BD, BD))
        base = energy[b] * corr[b].astype(F32)
        rows = []
        for i in range(16):
            rows.append(jnp.concatenate([parts[2 * i, b], parts[2 * i + 1, b]], axis=1))
        summed = jnp.concatenate(rows, axis=0).astype(F32)
        out[b] = jnp.where(mask, summed + base, 0.0)


def params(mib):
    return pltpu.CompilerParams(vmem_limit_bytes=mib * MIB)


def shape(dims, kind=BF):
    return jax.ShapeDtypeStruct(dims, kind)


def shards(wave_blocks, left_env, right_env, source, block_dims, energy):
    blk = lax.axis_index("blk").astype(jnp.int32)
    ids = blk[None]
    steps = left_env.shape[0] // STEP
    env = pl.BlockSpec((STEP, 4, BD, BD), lambda s: (s, 0, 0, 0))

    own = pl.pallas_call(
        pack_kernel,
        out_shape=shape((ROWS, BD)),
        in_specs=[SMEM, SMEM, VMEM],
        out_specs=VMEM,
        compiler_params=params(16),
        name="pack",
    )(block_dims, energy, wave_blocks)
    far = lax.ppermute(own, ALL, cross_pairs())
    core = lax.ppermute(own, "blk", core_pairs())
    far_core = lax.ppermute(far, "blk", core_pairs())

    partial = pl.pallas_call(
        wave_kernel,
        grid=(steps,),
        out_shape=shape((4, BD, BD)),
        in_specs=[SMEM, SMEM, VMEM, VMEM, VMEM, VMEM, env, env],
        out_specs=VMEM,
        scratch_shapes=[pltpu.VMEM((16, BD, BD), BF), pltpu.VMEM((4, BD, BD), F32)],
        compiler_params=params(32),
        name="wave_terms",
    )(source, ids, own, far, core, far_core, left_env, right_env)

    pieces = lax.all_to_all(partial.reshape(32, 32, BD), "op", 0, 0, tiled=True)
    copies = pl.pallas_call(
        reduce_kernel,
        out_shape=shape((64, 32, BD)),
        in_specs=[VMEM],
        out_specs=VMEM,
        compiler_params=params(16),
        name="sum_wave",
    )(pieces)
    same = lax.all_to_all(
        copies, ALL, 0, 0, tiled=True, axis_index_groups=core_groups()
    )
    other = lax.ppermute(same, "blk", core_pairs())

    applied_wave, corr, partial = pl.pallas_call(
        corr_kernel,
        grid=(steps,),
        out_shape=(shape((4, BD, BD), F32), shape((4, BD, BD)), shape((32, 4, 16, 128))),
        in_specs=[SMEM, SMEM] + [VMEM] * 6 + [env, env],
        out_specs=(VMEM, VMEM, VMEM),
        scratch_shapes=[
            pltpu.VMEM((16, BD, BD), BF),
            pltpu.VMEM((4, BD, BD), F32),
            pltpu.VMEM((16, BD, BD), F32),
        ],
        compiler_params=params(40),
        name="corr_terms",
    )(
        source, ids, own, far, core, far_core,
        same.reshape(2, 4, BD, BD), other.reshape(2, 4, BD, BD), left_env, right_env,
    )

    pieces = lax.all_to_all(partial.reshape(128, 16, 128), ALL, 0, 0, tiled=True)
    copies = pl.pallas_call(
        reduce_blocks_kernel,
        out_shape=shape((32, 4, 16, 128)),
        in_specs=[VMEM],
        out_specs=VMEM,
        compiler_params=params(16),
        name="sum_corr",
    )(pieces.reshape(32, 4, 16, 128))
    gathered = lax.all_to_all(copies, "op", 0, 0, tiled=True)
    applied_corr = pl.pallas_call(
        final_kernel,
        out_shape=shape((4, BD, BD), F32),
        in_specs=[SMEM, SMEM, VMEM, VMEM],
        out_specs=VMEM,
        compiler_params=params(16),
        name="finish",
    )(block_dims, energy, gathered, corr)
    return (applied_wave, applied_corr)


def solution(mesh):
    placed = (
        P("blk", None, None),
        P("op", "blk", None, None),
        P("op", "blk", None, None),
        P("op", "blk"),
        P(None, "blk"),
        P("blk"),
    )
    return jax.shard_map(
        shards,
        mesh=mesh,
        in_specs=placed,
        out_specs=(P("blk", None, None), P("blk", None, None)),
        check_vma=False,
    )
```

```python
import jax
import jax.numpy as jnp
from jax import lax
from jax.experimental import pallas as pl
from jax.experimental.pallas import tpu as pltpu
from jax.sharding import PartitionSpec as P

BF = jnp.bfloat16
F32 = jnp.float32
BD = 256
INFO = 32
ROWS = 4 * BD + INFO
BATCH = 8
CHUNKS = (4, 4, 4, 2, 2)
STRIP = 32
MIB = 1 << 20
ALL = ("op", "blk")

SMEM = pl.BlockSpec(memory_space=pltpu.SMEM)
VMEM = pl.BlockSpec(memory_space=pltpu.VMEM)
HBM = pl.BlockSpec(memory_space=pltpu.HBM)


def device(op, blk):
    return op * 4 + blk


def cross_pairs():
    return [(device(o, b), device(o ^ 16, b ^ 2)) for o in range(32) for b in range(4)]


def core_pairs():
    return [(b, b ^ 1) for b in range(4)]


def core_groups():
    return [[device(o, zh * 2 + c) for zh in range(2) for o in range(32)] for c in range(2)]


def live(rows, cols, shape, first_row=0, first_col=0):
    row_ids = lax.broadcasted_iota(jnp.int32, shape, 0) + first_row
    col_ids = lax.broadcasted_iota(jnp.int32, shape, 1) + first_col
    return (row_ids < rows) & (col_ids < cols)


def pack_kernel(dims_in, energy_in, wave_in, out, dims, energy, wave, sems):
    copies = [
        pltpu.make_async_copy(dims_in, dims, sems.at[0]),
        pltpu.make_async_copy(energy_in, energy, sems.at[1]),
        pltpu.make_async_copy(wave_in, wave, sems.at[2]),
    ]
    for copy in copies:
        copy.start()
    for copy in copies:
        copy.wait()
    for b in range(4):
        mask = live(dims[0, b], dims[1, b], (BD, BD))
        block = jnp.where(mask, wave[b].astype(F32), 0.0)
        out[b * BD:(b + 1) * BD, :] = block.astype(BF)
    row = lax.broadcasted_iota(jnp.int32, (INFO, BD), 0)
    info = jnp.zeros((INFO, BD), F32)
    for b in range(4):
        value = jnp.full((INFO, BD), energy[b], F32)
        high = value.astype(BF).astype(F32)
        middle = (value - high).astype(BF).astype(F32)
        low = value - high - middle
        parts = (dims[0, b].astype(F32), dims[1, b].astype(F32), high, middle, low)
        for j, part in enumerate(parts):
            info = jnp.where(row == b * 8 + j, part, info)
    out[4 * BD:, :] = info.astype(BF)


def slot_terms(src, vec, left, right, e, terms):
    inner = [
        jnp.dot(left[t, e], vec[src[e, t]], preferred_element_type=F32).astype(BF)
        for t in terms
    ]
    return lax.dot_general(
        jnp.concatenate(inner, axis=1),
        jnp.concatenate([right[t, e] for t in terms], axis=1),
        (((1,), (1,)), ((), ())),
        preferred_element_type=F32,
    )


def add_terms(src, vec, left, right, acc):
    acc[...] = jnp.zeros_like(acc)

    @pl.loop(0, left.shape[0] // BATCH)
    def _(step):
        terms = [step * BATCH + t for t in range(BATCH)]
        for e in range(4):
            acc[e] += slot_terms(src, vec, left, right, e, terms)


def wave_kernel(
    src_in, ids, own, far, core, far_core, left_in, right_in,
    out, vec, info, left, right, src, acc, src_sem, sems,
):
    src_copy = pltpu.make_async_copy(src_in, src, src_sem)
    src_copy.start()
    starts = [sum(CHUNKS[:i]) for i in range(len(CHUNKS))]
    chunks = []
    for i, (start, size) in enumerate(zip(starts, CHUNKS)):
        terms = pl.ds(start, size)
        chunks.append([
            pltpu.make_async_copy(left_in.at[terms], left.at[terms], sems.at[0, i]),
            pltpu.make_async_copy(right_in.at[terms], right.at[terms], sems.at[1, i]),
        ])
    for copies in chunks:
        for copy in copies:
            copy.start()
    for flip, piece in ((0, own), (2, far), (1, core), (3, far_core)):
        group = ids[0] ^ flip
        rows = piece[4 * BD:, :].astype(F32)
        for b in range(4):
            vec[group * 4 + b] = piece[b * BD:(b + 1) * BD, :]
            entry = rows[b * 8:(b + 1) * 8, :]
            level = entry[2:3] + entry[3:4] + entry[4:5]
            info[group * 4 + b, 0:2] = entry[0:2]
            info[group * 4 + b, 2:3] = level
    src_copy.wait()
    for i, copies in enumerate(chunks):
        for copy in copies:
            copy.wait()
        terms = range(starts[i], starts[i] + CHUNKS[i])
        for e in range(4):
            product = slot_terms(src, vec, left, right, e, terms)
            total = product if i == 0 else acc[e] + product
            if i == len(chunks) - 1:
                out[e] = total.astype(BF)
            else:
                acc[e] = total


def total_of(x):
    return jnp.sum(jnp.sum(x, axis=1, keepdims=True), axis=0, keepdims=True)


def fold(x):
    return jnp.sum(x.reshape(STRIP // 8, 8, BD), axis=0)


def corr_kernel(
    src, ids, wave, info, same, other, left, right,
    applied_out, corr_out, out, vec, acc, work,
):
    entries = 16 * BD * BD
    me = ids[0]
    zero = jnp.zeros((8, BD), F32)
    strips = [pl.ds(r, STRIP) for r in range(0, BD, STRIP)]

    def apply(group, sums):
        cross, square = sums
        for turn in range(4):
            b = me ^ turn
            summed = same if turn % 2 == 0 else other
            block = group * 4 + b
            level = info[block, 2:3]
            for rows in strips:
                vector = wave[block, rows].astype(F32)
                applied = summed[b >> 1, group, rows].astype(F32) + level * vector
                work[block, rows] = applied
                cross += fold(applied * vector)
                square += fold(vector * vector)
        return cross, square

    cross, square = lax.fori_loop(0, 4, apply, (zero, zero))
    for b in range(4):
        applied_out[b] = work[me * 4 + b]
    rayleigh = total_of(cross) / entries / (total_of(square) / entries + 1e-06)

    def subtract(group, resid):
        for b in range(4):
            for rows in strips:
                vector = wave[group * 4 + b, rows].astype(F32)
                rest = work[group * 4 + b, rows] - rayleigh * vector
                work[group * 4 + b, rows] = rest
                resid += fold(rest * rest)
        return resid

    resid = lax.fori_loop(0, 4, subtract, zero)
    scale = lax.rsqrt(total_of(resid) / entries + 1e-06)

    @pl.loop(0, 4)
    def _(group):
        for b in range(4):
            for rows in strips:
                vec[group * 4 + b, rows] = (work[group * 4 + b, rows] * scale).astype(BF)

    for b in range(4):
        corr_out[b] = vec[me * 4 + b]

    add_terms(src, vec, left, right, acc)
    for e in range(4):
        for i in range(16):
            for j in range(2):
                tile = acc[e, i * 16:(i + 1) * 16, j * 128:(j + 1) * 128]
                out[i * 2 + j, e] = tile.astype(BF)


def sum_wave_kernel(ids, info, parts, out):
    part = ids[1]
    entry = info[(part >> 3) * 4 + ids[0]]
    mask = live(entry[0:1], entry[1:2], (STRIP, BD), (part & 7) * STRIP)
    total = jnp.sum(parts[...].astype(F32), axis=0)
    total = jnp.where(mask, total, 0.0).astype(BF)
    for i in range(out.shape[0]):
        out[i] = total


def sum_corr_kernel(ids, info, parts, out):
    part = ids[1]
    totals = []
    for b in range(4):
        entry = info[ids[0] * 4 + b][:, :128]
        total = jnp.sum(parts[:, b].astype(F32), axis=0)
        mask = live(entry[0:1], entry[1:2], (16, 128), (part >> 1) * 16, (part & 1) * 128)
        totals.append(jnp.where(mask, total, 0.0).astype(BF))
    for i in range(out.shape[0]):
        for b in range(4):
            out[i, b] = totals[b]


def final_kernel(ids, info, parts, corr, out):
    for b in range(4):
        level = info[ids[0] * 4 + b, 2:3]
        for i in range(16):
            rows = pl.ds(i * 16, 16)
            summed = jnp.concatenate([parts[2 * i, b], parts[2 * i + 1, b]], axis=1)
            out[b, rows] = summed.astype(F32) + level * corr[b, rows].astype(F32)


def params(mib):
    return pltpu.CompilerParams(vmem_limit_bytes=mib * MIB)


def shape(dims, kind=BF):
    return jax.ShapeDtypeStruct(dims, kind)


def shards(wave_blocks, left_env, right_env, source, block_dims, energy):
    ids = jnp.stack([lax.axis_index("blk"), lax.axis_index("op")]).astype(jnp.int32)
    src = source.T

    own = pl.pallas_call(
        pack_kernel,
        out_shape=shape((ROWS, BD)),
        in_specs=[HBM, HBM, HBM],
        out_specs=VMEM,
        scratch_shapes=[
            pltpu.SMEM((2, 4), jnp.int32),
            pltpu.SMEM((4,), F32),
            pltpu.VMEM((4, BD, BD), BF),
            pltpu.SemaphoreType.DMA((3,)),
        ],
        compiler_params=params(8),
        name="pack",
    )(*(pltpu.with_memory_space_constraint(x, pltpu.HBM) for x in (block_dims, energy, wave_blocks)))
    far = lax.ppermute(own, ALL, cross_pairs())
    core = lax.ppermute(own, "blk", core_pairs())
    far_core = lax.ppermute(far, "blk", core_pairs())

    partial, wave, info, left, right = pl.pallas_call(
        wave_kernel,
        out_shape=(
            shape((4, BD, BD)), shape((16, BD, BD)), shape((16, 8, BD), F32),
            pltpu.VMEM(left_env.shape, BF), pltpu.VMEM(right_env.shape, BF),
        ),
        in_specs=[HBM, SMEM] + [VMEM] * 4 + [HBM, HBM],
        out_specs=(VMEM,) * 5,
        scratch_shapes=[
            pltpu.SMEM((4, 16), jnp.int32),
            pltpu.VMEM((4, BD, BD), F32),
            pltpu.SemaphoreType.DMA,
            pltpu.SemaphoreType.DMA((2, len(CHUNKS))),
        ],
        compiler_params=params(14),
        name="wave_terms",
    )(
        pltpu.with_memory_space_constraint(src, pltpu.HBM), ids, own, far, core, far_core,
        pltpu.with_memory_space_constraint(left_env, pltpu.HBM),
        pltpu.with_memory_space_constraint(right_env, pltpu.HBM),
    )

    pieces = lax.all_to_all(partial.reshape(32, 32, BD), "op", 0, 0, tiled=True)
    copies = pl.pallas_call(
        sum_wave_kernel,
        out_shape=shape((64, 32, BD)),
        in_specs=[SMEM, VMEM, VMEM],
        out_specs=VMEM,
        compiler_params=params(8),
        name="sum_wave",
    )(ids, info, pieces)
    same = lax.all_to_all(
        copies, ALL, 0, 0, tiled=True, axis_index_groups=core_groups()
    )
    other = lax.ppermute(same, "blk", core_pairs())

    applied_wave, corr, partial = pl.pallas_call(
        corr_kernel,
        out_shape=(shape((4, BD, BD), F32), shape((4, BD, BD)), shape((32, 4, 16, 128))),
        in_specs=[SMEM, SMEM] + [VMEM] * 6,
        out_specs=(VMEM, VMEM, VMEM),
        scratch_shapes=[
            pltpu.VMEM((16, BD, BD), BF),
            pltpu.VMEM((4, BD, BD), F32),
            pltpu.VMEM((16, BD, BD), F32),
        ],
        compiler_params=params(14),
        name="corr_terms",
    )(
        src, ids, wave, info,
        same.reshape(2, 4, BD, BD), other.reshape(2, 4, BD, BD), left, right,
    )

    pieces = lax.all_to_all(partial.reshape(128, 16, 128), ALL, 0, 0, tiled=True)
    copies = pl.pallas_call(
        sum_corr_kernel,
        out_shape=shape((32, 4, 16, 128)),
        in_specs=[SMEM, VMEM, VMEM],
        out_specs=VMEM,
        compiler_params=params(8),
        name="sum_corr",
    )(ids, info, pieces.reshape(32, 4, 16, 128))
    gathered = lax.all_to_all(copies, "op", 0, 0, tiled=True)
    applied_corr = pl.pallas_call(
        final_kernel,
        out_shape=shape((4, BD, BD), F32),
        in_specs=[SMEM, VMEM, VMEM, VMEM],
        out_specs=VMEM,
        compiler_params=params(8),
        name="finish",
    )(ids, info, gathered, corr)
    return (applied_wave, applied_corr)


def solution(mesh):
    placed = (
        P("blk", None, None),
        P("op", "blk", None, None),
        P("op", "blk", None, None),
        P("op", "blk"),
        P(None, "blk"),
        P("blk"),
    )
    return jax.shard_map(
        shards,
        mesh=mesh,
        in_specs=placed,
        out_specs=(P("blk", None, None), P("blk", None, None)),
        check_vma=False,
    )
```

```python
import jax
import jax.numpy as jnp
from jax import lax
from jax.experimental import pallas as pl
from jax.experimental.pallas import tpu as pltpu
from jax.sharding import PartitionSpec as P

BF = jnp.bfloat16
F32 = jnp.float32
BD = 256
INFO = 16
ROWS = BD + INFO
BATCH = 8
CHUNKS = (4, 4, 4, 2, 2)
STRIP = 32
MIB = 1 << 20
ALL = ("op", "blk")

SMEM = pl.BlockSpec(memory_space=pltpu.SMEM)
VMEM = pl.BlockSpec(memory_space=pltpu.VMEM)
HBM = pl.BlockSpec(memory_space=pltpu.HBM)


def device(op, blk):
    return op * 4 + blk


def cross_pairs():
    return [(device(o, b), device(o ^ 16, b ^ 2)) for o in range(32) for b in range(4)]


def flip_pairs(bit):
    return [(o, o ^ bit) for o in range(32)]


def color_of(op):
    x, y, z = op & 1, (op >> 2) & 1, op >> 4
    return (x ^ z) + 2 * (y ^ z)


def core_pairs():
    return [(b, b ^ 1) for b in range(4)]


def core_groups():
    return [[device(o, zh * 2 + c) for zh in range(2) for o in range(32)] for c in range(2)]


def live(rows, cols, shape, first_row=0, first_col=0):
    row_ids = lax.broadcasted_iota(jnp.int32, shape, 0) + first_row
    col_ids = lax.broadcasted_iota(jnp.int32, shape, 1) + first_col
    return (row_ids < rows) & (col_ids < cols)


def pack_kernel(dims_in, energy_in, wave_in, out, first, dims, energy, wave, sems):
    copies = [
        pltpu.make_async_copy(dims_in, dims, sems.at[0]),
        pltpu.make_async_copy(energy_in, energy, sems.at[1]),
        pltpu.make_async_copy(wave_in, wave, sems.at[2]),
    ]
    for copy in copies:
        copy.start()
    for copy in copies:
        copy.wait()
    row = lax.broadcasted_iota(jnp.int32, (INFO, BD), 0)
    for b in range(4):
        mask = live(dims[0, b], dims[1, b], (BD, BD))
        out[b, :BD] = jnp.where(mask, wave[b].astype(F32), 0.0).astype(BF)
        value = jnp.full((INFO, BD), energy[b], F32)
        high = value.astype(BF).astype(F32)
        middle = (value - high).astype(BF).astype(F32)
        low = value - high - middle
        info = jnp.zeros((INFO, BD), F32)
        parts = (dims[0, b].astype(F32), dims[1, b].astype(F32), high, middle, low)
        for j, part in enumerate(parts):
            info = jnp.where(row == j, part, info)
        out[b, BD:] = info.astype(BF)
    first[...] = out[color_of(lax.axis_index("op")) ^ 3]


def slot_terms(src, vec, left, right, e, terms):
    inner = [
        jnp.dot(left[t, e], vec[src[e, t]], preferred_element_type=F32).astype(BF)
        for t in terms
    ]
    return lax.dot_general(
        jnp.concatenate(inner, axis=1),
        jnp.concatenate([right[t, e] for t in terms], axis=1),
        (((1,), (1,)), ((), ())),
        preferred_element_type=F32,
    )


def add_terms(src, vec, left, right, acc):
    acc[...] = jnp.zeros_like(acc)

    @pl.loop(0, left.shape[0] // BATCH)
    def _(step):
        terms = [step * BATCH + t for t in range(BATCH)]
        for e in range(4):
            acc[e] += slot_terms(src, vec, left, right, e, terms)


def wave_kernel(
    src_in, own, core, far0, far1, far2, far3, near0, near1, near2, near3,
    left_in, right_in, out, vec, info, left, right, src, acc, src_sem, sems,
):
    src_copy = pltpu.make_async_copy(src_in, src, src_sem)
    src_copy.start()
    starts = [sum(CHUNKS[:i]) for i in range(len(CHUNKS))]
    chunks = []
    for i, (start, size) in enumerate(zip(starts, CHUNKS)):
        terms = pl.ds(start, size)
        chunks.append([
            pltpu.make_async_copy(left_in.at[terms], left.at[terms], sems.at[0, i]),
            pltpu.make_async_copy(right_in.at[terms], right.at[terms], sems.at[1, i]),
        ])
    for copies in chunks:
        for copy in copies:
            copy.start()
    blocks = []
    for b in range(4):
        blocks.append((lax.axis_index("blk") * 4 + b, own.at[b]))
        blocks.append(((lax.axis_index("blk") ^ 1) * 4 + b, core.at[b]))
    for flip, pieces in ((2, (far0, far1, far2, far3)), (3, (near0, near1, near2, near3))):
        for b, piece in enumerate(pieces):
            blocks.append(((lax.axis_index("blk") ^ flip) * 4 + (color_of(lax.axis_index("op")) ^ b), piece))
    for block, piece in blocks:
        vec[block] = piece[:BD]
        entry = piece[BD:].astype(F32)
        info[block, 0:2] = entry[0:2]
        info[block, 2:3] = entry[2:3] + entry[3:4] + entry[4:5]
    src_copy.wait()
    for i, copies in enumerate(chunks):
        for copy in copies:
            copy.wait()
        terms = range(starts[i], starts[i] + CHUNKS[i])
        for e in range(4):
            product = slot_terms(src, vec, left, right, e, terms)
            total = product if i == 0 else acc[e] + product
            if i == len(chunks) - 1:
                out[e] = total.astype(BF)
            else:
                acc[e] = total


def total_of(x):
    return jnp.sum(jnp.sum(x, axis=1, keepdims=True), axis=0, keepdims=True)


def fold(x):
    return jnp.sum(x.reshape(STRIP // 8, 8, BD), axis=0)


def corr_kernel(
    src, wave, info, same, other, left, right,
    applied_out, corr_out, out, vec, acc, work, applied, applied_sem,
):
    entries = 16 * BD * BD
    me = lax.axis_index("blk")
    zero = jnp.zeros((8, BD), F32)
    strips = [pl.ds(r, STRIP) for r in range(0, BD, STRIP)]

    def summed(group, turn):
        b = me ^ turn
        return b, (same if turn % 2 == 0 else other).at[b >> 1, group]

    def cross_sums(group, sums):
        cross, square = sums
        for turn in range(4):
            b, values = summed(group, turn)
            block = group * 4 + b
            part, own_part = zero, zero
            for rows in strips:
                vector = wave[block, rows].astype(F32)
                part += fold(values[rows].astype(F32) * vector)
                own_part += fold(vector * vector)
            cross += part + info[block, 2:3] * own_part
            square += own_part
        return cross, square

    cross, square = lax.fori_loop(0, 4, cross_sums, (zero, zero))
    rayleigh = total_of(cross) / entries / (total_of(square) / entries + 1e-06)

    def subtract(group, resid):
        for turn in range(4):
            b, values = summed(group, turn)
            block = group * 4 + b
            level = info[block, 2:3] - rayleigh
            for rows in strips:
                rest = values[rows].astype(F32) + level * wave[block, rows].astype(F32)
                work[block, rows] = rest
                resid += fold(rest * rest)
        return resid

    resid = lax.fori_loop(0, 4, subtract, zero)
    scale = lax.rsqrt(total_of(resid) / entries + 1e-06)
    for turn in range(4):
        b, values = summed(me, turn)
        level = info[me * 4 + b, 2:3]
        for rows in strips:
            vector = wave[me * 4 + b, rows].astype(F32)
            applied[b, rows] = values[rows].astype(F32) + level * vector

    applied_copy = pltpu.make_async_copy(applied, applied_out, applied_sem)
    applied_copy.start()

    @pl.loop(0, 4)
    def _(group):
        for b in range(4):
            for rows in strips:
                vec[group * 4 + b, rows] = (work[group * 4 + b, rows] * scale).astype(BF)

    for b in range(4):
        corr_out[b] = vec[me * 4 + b]

    add_terms(src, vec, left, right, acc)
    for e in range(4):
        for i in range(16):
            for j in range(2):
                tile = acc[e, i * 16:(i + 1) * 16, j * 128:(j + 1) * 128]
                out[i * 2 + j, e] = tile.astype(BF)
    applied_copy.wait()


def sum_wave_kernel(info, parts, out):
    part = lax.axis_index("op")
    entry = info[(part >> 3) * 4 + lax.axis_index("blk")]
    mask = live(entry[0:1], entry[1:2], (STRIP, BD), (part & 7) * STRIP)
    total = jnp.sum(parts[...].astype(F32), axis=0)
    total = jnp.where(mask, total, 0.0).astype(BF)
    for i in range(out.shape[0]):
        out[i] = total


def sum_corr_kernel(info, parts, out):
    part = lax.axis_index("op")
    totals = []
    for b in range(4):
        entry = info[lax.axis_index("blk") * 4 + b][:, :128]
        total = jnp.sum(parts[:, b].astype(F32), axis=0)
        mask = live(entry[0:1], entry[1:2], (16, 128), (part >> 1) * 16, (part & 1) * 128)
        totals.append(jnp.where(mask, total, 0.0).astype(BF))
    for i in range(out.shape[0]):
        for b in range(4):
            out[i, b] = totals[b]


def final_kernel(info, parts, corr, out, blocks, sems):
    copies = []
    for b in range(4):
        level = info[lax.axis_index("blk") * 4 + b, 2:3]
        for i in range(16):
            rows = pl.ds(i * 16, 16)
            summed = jnp.concatenate([parts[2 * i, b], parts[2 * i + 1, b]], axis=1)
            blocks[b, rows] = summed.astype(F32) + level * corr[b, rows].astype(F32)
        copies.append(pltpu.make_async_copy(blocks.at[b], out.at[b], sems.at[b]))
        copies[b].start()
    for copy in copies:
        copy.wait()


def params(mib):
    return pltpu.CompilerParams(vmem_limit_bytes=mib * MIB)


def shape(dims, kind=BF):
    return jax.ShapeDtypeStruct(dims, kind)


def shards(wave_blocks, left_env, right_env, source, block_dims, energy):
    src = source.T

    own, first = pl.pallas_call(
        pack_kernel,
        out_shape=(shape((4, ROWS, BD)), shape((ROWS, BD))),
        in_specs=[HBM, HBM, HBM],
        out_specs=(VMEM, VMEM),
        scratch_shapes=[
            pltpu.SMEM((2, 4), jnp.int32),
            pltpu.SMEM((4,), F32),
            pltpu.VMEM((4, BD, BD), BF),
            pltpu.SemaphoreType.DMA((3,)),
        ],
        compiler_params=params(8),
        name="pack",
    )(*(pltpu.with_memory_space_constraint(x, pltpu.HBM) for x in (block_dims, energy, wave_blocks)))
    far = [lax.ppermute(first, ALL, cross_pairs())]
    core = lax.ppermute(own, "blk", core_pairs())
    for bit in (1, 4, 16):
        far.append(lax.ppermute(far[0], "op", flip_pairs(bit)))
    near = [lax.ppermute(piece, "blk", core_pairs()) for piece in far]

    partial, wave, info, left, right = pl.pallas_call(
        wave_kernel,
        out_shape=(
            shape((4, BD, BD)), shape((16, BD, BD)), shape((16, 8, BD), F32),
            pltpu.VMEM(left_env.shape, BF), pltpu.VMEM(right_env.shape, BF),
        ),
        in_specs=[HBM] + [VMEM] * 10 + [HBM, HBM],
        out_specs=(VMEM,) * 5,
        scratch_shapes=[
            pltpu.SMEM((4, 16), jnp.int32),
            pltpu.VMEM((4, BD, BD), F32),
            pltpu.SemaphoreType.DMA,
            pltpu.SemaphoreType.DMA((2, len(CHUNKS))),
        ],
        compiler_params=params(14),
        name="wave_terms",
    )(
        pltpu.with_memory_space_constraint(src, pltpu.HBM), own, core, *far, *near,
        pltpu.with_memory_space_constraint(left_env, pltpu.HBM),
        pltpu.with_memory_space_constraint(right_env, pltpu.HBM),
    )

    pieces = lax.all_to_all(partial.reshape(32, 32, BD), "op", 0, 0, tiled=True)
    copies = pl.pallas_call(
        sum_wave_kernel,
        out_shape=shape((64, 32, BD)),
        in_specs=[VMEM, VMEM],
        out_specs=VMEM,
        compiler_params=params(8),
        name="sum_wave",
    )(info, pieces)
    same = lax.all_to_all(
        copies, ALL, 0, 0, tiled=True, axis_index_groups=core_groups()
    )
    other = lax.ppermute(same, "blk", core_pairs())

    applied_wave, corr, partial = pl.pallas_call(
        corr_kernel,
        out_shape=(shape((4, BD, BD), F32), shape((4, BD, BD)), shape((32, 4, 16, 128))),
        in_specs=[SMEM] + [VMEM] * 6,
        out_specs=(HBM, VMEM, VMEM),
        scratch_shapes=[
            pltpu.VMEM((16, BD, BD), BF),
            pltpu.VMEM((4, BD, BD), F32),
            pltpu.VMEM((16, BD, BD), F32),
            pltpu.VMEM((4, BD, BD), F32),
            pltpu.SemaphoreType.DMA,
        ],
        compiler_params=params(14),
        name="corr_terms",
    )(
        src, wave, info,
        same.reshape(2, 4, BD, BD), other.reshape(2, 4, BD, BD), left, right,
    )

    pieces = lax.all_to_all(partial.reshape(128, 16, 128), ALL, 0, 0, tiled=True)
    copies = pl.pallas_call(
        sum_corr_kernel,
        out_shape=shape((32, 4, 16, 128)),
        in_specs=[VMEM, VMEM],
        out_specs=VMEM,
        compiler_params=params(8),
        name="sum_corr",
    )(info, pieces.reshape(32, 4, 16, 128))
    gathered = lax.all_to_all(copies, "op", 0, 0, tiled=True)
    applied_corr = pl.pallas_call(
        final_kernel,
        out_shape=shape((4, BD, BD), F32),
        in_specs=[VMEM, VMEM, VMEM],
        out_specs=HBM,
        scratch_shapes=[pltpu.VMEM((4, BD, BD), F32), pltpu.SemaphoreType.DMA((4,))],
        compiler_params=params(8),
        name="finish",
    )(info, gathered, corr)
    return (applied_wave, applied_corr)


def solution(mesh):
    placed = (
        P("blk", None, None),
        P("op", "blk", None, None),
        P("op", "blk", None, None),
        P("op", "blk"),
        P(None, "blk"),
        P("blk"),
    )
    return jax.shard_map(
        shards,
        mesh=mesh,
        in_specs=placed,
        out_specs=(P("blk", None, None), P("blk", None, None)),
        check_vma=False,
    )
```

```python
import jax
import jax.numpy as jnp
from jax import lax
from jax.experimental import pallas as pl
from jax.experimental.pallas import tpu as pltpu
from jax.sharding import PartitionSpec as P

BF = jnp.bfloat16
F32 = jnp.float32
BD = 256
INFO = 16
ROWS = BD + INFO
HALF = 8
STRIP = 32
MIB = 1 << 20
ALL = ("op", "blk")

SMEM = pl.BlockSpec(memory_space=pltpu.SMEM)
VMEM = pl.BlockSpec(memory_space=pltpu.VMEM)
HBM = pl.BlockSpec(memory_space=pltpu.HBM)


def device(op, blk):
    return op * 4 + blk


def cross_pairs():
    return [(device(o, b), device(o ^ 16, b ^ 2)) for o in range(32) for b in range(4)]


def flip_pairs(bit):
    return [(o, o ^ bit) for o in range(32)]


def color_of(op):
    x, y, z = op & 1, (op >> 2) & 1, op >> 4
    return (x ^ z) + 2 * (y ^ z)


def core_pairs():
    return [(b, b ^ 1) for b in range(4)]


def core_groups():
    return [[device(o, zh * 2 + c) for zh in range(2) for o in range(32)] for c in range(2)]


def live(rows, cols, shape, first_row=0, first_col=0):
    row_ids = lax.broadcasted_iota(jnp.int32, shape, 0) + first_row
    col_ids = lax.broadcasted_iota(jnp.int32, shape, 1) + first_col
    return (row_ids < rows) & (col_ids < cols)


def pack_kernel(dims_in, energy_in, wave_in, out, first, dims, energy, wave, sems):
    copies = [
        pltpu.make_async_copy(dims_in, dims, sems.at[0]),
        pltpu.make_async_copy(energy_in, energy, sems.at[1]),
        pltpu.make_async_copy(wave_in, wave, sems.at[2]),
    ]
    for copy in copies:
        copy.start()
    for copy in copies:
        copy.wait()
    row = lax.broadcasted_iota(jnp.int32, (INFO, BD), 0)
    for b in range(4):
        mask = live(dims[0, b], dims[1, b], (BD, BD))
        out[b, :BD] = jnp.where(mask, wave[b].astype(F32), 0.0).astype(BF)
        value = jnp.full((INFO, BD), energy[b], F32)
        high = value.astype(BF).astype(F32)
        middle = (value - high).astype(BF).astype(F32)
        low = value - high - middle
        info = jnp.zeros((INFO, BD), F32)
        parts = (dims[0, b].astype(F32), dims[1, b].astype(F32), high, middle, low)
        for j, part in enumerate(parts):
            info = jnp.where(row == j, part, info)
        out[b, BD:] = info.astype(BF)
    first[...] = out[color_of(lax.axis_index("op")) ^ 3]


def load_kernel(left, right, left_out, right_out, token, sems):
    copies = [
        pltpu.make_async_copy(left, left_out, sems.at[0]),
        pltpu.make_async_copy(right.at[pl.ds(0, HALF)], right_out, sems.at[1]),
    ]
    for copy in copies:
        copy.start()
    token[...] = jnp.zeros_like(token)
    for copy in copies:
        copy.wait()


def slot_terms(src, vec, left, right, e, first):
    inner = [
        jnp.dot(left[first + t, e], vec[src[e, first + t]], preferred_element_type=F32).astype(BF)
        for t in range(HALF)
    ]
    return lax.dot_general(
        jnp.concatenate(inner, axis=1),
        jnp.concatenate([right[t, e] for t in range(HALF)], axis=1),
        (((1,), (1,)), ((), ())),
        preferred_element_type=F32,
    )


def wave_kernel(
    src_in, own, core, far0, far1, far2, far3, near0, near1, near2, near3,
    left, right_a, right_in, token, out, vec, info, right_b, src, acc, src_sem, sem,
):
    src_copy = pltpu.make_async_copy(src_in, src, src_sem)
    src_copy.start()
    right_copy = pltpu.make_async_copy(right_in.at[pl.ds(HALF, HALF)], right_b, sem)
    right_copy.start()
    me, color = lax.axis_index("blk"), color_of(lax.axis_index("op"))
    blocks = []
    for b in range(4):
        blocks.append((me * 4 + b, own.at[b]))
        blocks.append(((me ^ 1) * 4 + b, core.at[b]))
    for flip, pieces in ((2, (far0, far1, far2, far3)), (3, (near0, near1, near2, near3))):
        for b, piece in enumerate(pieces):
            blocks.append(((me ^ flip) * 4 + (color ^ b), piece))
    for block, piece in blocks:
        vec[block] = piece[:BD]
        entry = piece[BD:].astype(F32)
        info[block, 0:2] = entry[0:2]
        info[block, 2:3] = entry[2:3] + entry[3:4] + entry[4:5]
    src_copy.wait()
    for e in range(4):
        acc[e] = slot_terms(src, vec, left, right_a, e, 0)
    right_copy.wait()
    for e in range(4):
        out[e] = (acc[e] + slot_terms(src, vec, left, right_b, e, HALF)).astype(BF)


def total_of(x):
    return jnp.sum(jnp.sum(x, axis=1, keepdims=True), axis=0, keepdims=True)


def fold(x):
    return jnp.sum(x.reshape(STRIP // 8, 8, BD), axis=0)


def corr_kernel(
    src, wave, info, same, other, left, right_a, right_b,
    applied_out, corr_out, out, vec, acc, work, applied, applied_sem,
):
    entries = 16 * BD * BD
    me = lax.axis_index("blk")
    zero = jnp.zeros((8, BD), F32)
    strips = [pl.ds(r, STRIP) for r in range(0, BD, STRIP)]

    def summed(group, turn):
        b = me ^ turn
        return b, (same if turn % 2 == 0 else other).at[b >> 1, group]

    def cross_sums(group, sums):
        cross, square = sums
        for turn in range(4):
            b, values = summed(group, turn)
            block = group * 4 + b
            part, own_part = zero, zero
            for rows in strips:
                vector = wave[block, rows].astype(F32)
                part += fold(values[rows].astype(F32) * vector)
                own_part += fold(vector * vector)
            cross += part + info[block, 2:3] * own_part
            square += own_part
        return cross, square

    cross, square = lax.fori_loop(0, 4, cross_sums, (zero, zero))
    rayleigh = total_of(cross) / entries / (total_of(square) / entries + 1e-06)

    def subtract(group, resid):
        for turn in range(4):
            b, values = summed(group, turn)
            block = group * 4 + b
            level = info[block, 2:3] - rayleigh
            for rows in strips:
                rest = values[rows].astype(F32) + level * wave[block, rows].astype(F32)
                work[block, rows] = rest
                resid += fold(rest * rest)
        return resid

    resid = lax.fori_loop(0, 4, subtract, zero)
    scale = lax.rsqrt(total_of(resid) / entries + 1e-06)
    for turn in range(4):
        b, values = summed(me, turn)
        level = info[me * 4 + b, 2:3]
        for rows in strips:
            vector = wave[me * 4 + b, rows].astype(F32)
            applied[b, rows] = values[rows].astype(F32) + level * vector

    applied_copy = pltpu.make_async_copy(applied, applied_out, applied_sem)
    applied_copy.start()

    @pl.loop(0, 4)
    def _(group):
        for b in range(4):
            for rows in strips:
                vec[group * 4 + b, rows] = (work[group * 4 + b, rows] * scale).astype(BF)

    for b in range(4):
        corr_out[b] = vec[me * 4 + b]

    for e in range(4):
        acc[e] = slot_terms(src, vec, left, right_a, e, 0)
    for e in range(4):
        total = acc[e] + slot_terms(src, vec, left, right_b, e, HALF)
        for i in range(16):
            for j in range(2):
                tile = total[i * 16:(i + 1) * 16, j * 128:(j + 1) * 128]
                out[i * 2 + j, e] = tile.astype(BF)
    applied_copy.wait()


def sum_wave_kernel(info, parts, out):
    part = lax.axis_index("op")
    entry = info[(part >> 3) * 4 + lax.axis_index("blk")]
    mask = live(entry[0:1], entry[1:2], (STRIP, BD), (part & 7) * STRIP)
    total = jnp.sum(parts[...].astype(F32), axis=0)
    total = jnp.where(mask, total, 0.0).astype(BF)
    for i in range(out.shape[0]):
        out[i] = total


def sum_corr_kernel(info, parts, out):
    part = lax.axis_index("op")
    totals = []
    for b in range(4):
        entry = info[lax.axis_index("blk") * 4 + b][:, :128]
        total = jnp.sum(parts[:, b].astype(F32), axis=0)
        mask = live(entry[0:1], entry[1:2], (16, 128), (part >> 1) * 16, (part & 1) * 128)
        totals.append(jnp.where(mask, total, 0.0).astype(BF))
    for i in range(out.shape[0]):
        for b in range(4):
            out[i, b] = totals[b]


def final_kernel(info, parts, corr, out, blocks, sems):
    copies = []
    for b in range(4):
        level = info[lax.axis_index("blk") * 4 + b, 2:3]
        for i in range(16):
            rows = pl.ds(i * 16, 16)
            summed = jnp.concatenate([parts[2 * i, b], parts[2 * i + 1, b]], axis=1)
            blocks[b, rows] = summed.astype(F32) + level * corr[b, rows].astype(F32)
        copies.append(pltpu.make_async_copy(blocks.at[b], out.at[b], sems.at[b]))
        copies[b].start()
    for copy in copies:
        copy.wait()


def params(mib):
    return pltpu.CompilerParams(vmem_limit_bytes=mib * MIB)


def shape(dims, kind=BF):
    return jax.ShapeDtypeStruct(dims, kind)


def shards(wave_blocks, left_env, right_env, source, block_dims, energy):
    src = source.T

    own, first = pl.pallas_call(
        pack_kernel,
        out_shape=(shape((4, ROWS, BD)), shape((ROWS, BD))),
        in_specs=[HBM, HBM, HBM],
        out_specs=(VMEM, VMEM),
        scratch_shapes=[
            pltpu.SMEM((2, 4), jnp.int32),
            pltpu.SMEM((4,), F32),
            pltpu.VMEM((4, BD, BD), BF),
            pltpu.SemaphoreType.DMA((3,)),
        ],
        compiler_params=params(8),
        name="pack",
    )(*(pltpu.with_memory_space_constraint(x, pltpu.HBM) for x in (block_dims, energy, wave_blocks)))
    far = [lax.ppermute(first, ALL, cross_pairs())]
    left_in, right_in = (
        pltpu.with_memory_space_constraint(x, pltpu.HBM) for x in (left_env, right_env)
    )
    half = (HALF,) + right_env.shape[1:]
    left, right_a, token = pl.pallas_call(
        load_kernel,
        out_shape=(pltpu.VMEM(left_env.shape, BF), pltpu.VMEM(half, BF), shape((8, 128), F32)),
        in_specs=[HBM, HBM],
        out_specs=(VMEM, VMEM, VMEM),
        scratch_shapes=[pltpu.SemaphoreType.DMA((2,))],
        compiler_params=params(1),
        name="load",
    )(left_in, right_in)
    far[0], token = lax.optimization_barrier((far[0], token))
    core = lax.ppermute(own, "blk", core_pairs())
    for bit in (1, 4, 16):
        far.append(lax.ppermute(far[0], "op", flip_pairs(bit)))
    near = [lax.ppermute(piece, "blk", core_pairs()) for piece in far]

    partial, wave, info, right_b = pl.pallas_call(
        wave_kernel,
        out_shape=(
            shape((4, BD, BD)), shape((16, BD, BD)), shape((16, 8, BD), F32), pltpu.VMEM(half, BF),
        ),
        in_specs=[HBM] + [VMEM] * 12 + [HBM, VMEM],
        out_specs=(VMEM,) * 4,
        scratch_shapes=[
            pltpu.SMEM((4, 16), jnp.int32),
            pltpu.VMEM((4, BD, BD), F32),
            pltpu.SemaphoreType.DMA,
            pltpu.SemaphoreType.DMA,
        ],
        compiler_params=params(8),
        name="wave_terms",
    )(
        pltpu.with_memory_space_constraint(src, pltpu.HBM), own, core, *far, *near,
        left, right_a, right_in, token,
    )

    pieces = lax.all_to_all(partial.reshape(32, 32, BD), "op", 0, 0, tiled=True)
    copies = pl.pallas_call(
        sum_wave_kernel,
        out_shape=shape((64, 32, BD)),
        in_specs=[VMEM, VMEM],
        out_specs=VMEM,
        compiler_params=params(8),
        name="sum_wave",
    )(info, pieces)
    same = lax.all_to_all(
        copies, ALL, 0, 0, tiled=True, axis_index_groups=core_groups()
    )
    other = lax.ppermute(same, "blk", core_pairs())

    applied_wave, corr, partial = pl.pallas_call(
        corr_kernel,
        out_shape=(shape((4, BD, BD), F32), shape((4, BD, BD)), shape((32, 4, 16, 128))),
        in_specs=[SMEM] + [VMEM] * 7,
        out_specs=(HBM, VMEM, VMEM),
        scratch_shapes=[
            pltpu.VMEM((16, BD, BD), BF),
            pltpu.VMEM((4, BD, BD), F32),
            pltpu.VMEM((16, BD, BD), F32),
            pltpu.VMEM((4, BD, BD), F32),
            pltpu.SemaphoreType.DMA,
        ],
        compiler_params=params(14),
        name="corr_terms",
    )(
        src, wave, info,
        same.reshape(2, 4, BD, BD), other.reshape(2, 4, BD, BD), left, right_a, right_b,
    )

    pieces = lax.all_to_all(partial.reshape(128, 16, 128), ALL, 0, 0, tiled=True)
    copies = pl.pallas_call(
        sum_corr_kernel,
        out_shape=shape((32, 4, 16, 128)),
        in_specs=[VMEM, VMEM],
        out_specs=VMEM,
        compiler_params=params(8),
        name="sum_corr",
    )(info, pieces.reshape(32, 4, 16, 128))
    gathered = lax.all_to_all(copies, "op", 0, 0, tiled=True)
    applied_corr = pl.pallas_call(
        final_kernel,
        out_shape=shape((4, BD, BD), F32),
        in_specs=[VMEM, VMEM, VMEM],
        out_specs=HBM,
        scratch_shapes=[pltpu.VMEM((4, BD, BD), F32), pltpu.SemaphoreType.DMA((4,))],
        compiler_params=params(8),
        name="finish",
    )(info, gathered, corr)
    return (applied_wave, applied_corr)


def solution(mesh):
    placed = (
        P("blk", None, None),
        P("op", "blk", None, None),
        P("op", "blk", None, None),
        P("op", "blk"),
        P(None, "blk"),
        P("blk"),
    )
    return jax.shard_map(
        shards,
        mesh=mesh,
        in_specs=placed,
        out_specs=(P("blk", None, None), P("blk", None, None)),
        check_vma=False,
    )
```

```python
import jax
import jax.numpy as jnp
from jax import lax
from jax.experimental import pallas as pl
from jax.experimental.pallas import tpu as pltpu
from jax.sharding import PartitionSpec as P

BF = jnp.bfloat16
F32 = jnp.float32
BD = 256
INFO = 16
ROWS = BD + INFO
HALF = 8
STRIP = 32
MIB = 1 << 20
ALL = ("op", "blk")

SMEM = pl.BlockSpec(memory_space=pltpu.SMEM)
VMEM = pl.BlockSpec(memory_space=pltpu.VMEM)
HBM = pl.BlockSpec(memory_space=pltpu.HBM)


def device(op, blk):
    return op * 4 + blk


def cross_pairs():
    return [(device(o, b), device(o ^ 16, b ^ 2)) for o in range(32) for b in range(4)]


def flip_pairs(bit):
    return [(o, o ^ bit) for o in range(32)]


def color_of(op):
    x, y, z = op & 1, (op >> 2) & 1, op >> 4
    return (x ^ z) + 2 * (y ^ z)


def core_pairs():
    return [(b, b ^ 1) for b in range(4)]


def core_groups():
    return [[device(o, zh * 2 + c) for zh in range(2) for o in range(32)] for c in range(2)]


def live(rows, cols, shape, first_row=0, first_col=0):
    row_ids = lax.broadcasted_iota(jnp.int32, shape, 0) + first_row
    col_ids = lax.broadcasted_iota(jnp.int32, shape, 1) + first_col
    return (row_ids < rows) & (col_ids < cols)


def pack(rows, cols, energy, wave):
    row = lax.broadcasted_iota(jnp.int32, (INFO, BD), 0)
    block = jnp.where(live(rows, cols, (BD, BD)), wave.astype(F32), 0.0)
    value = jnp.full((INFO, BD), energy, F32)
    high = value.astype(BF).astype(F32)
    middle = (value - high).astype(BF).astype(F32)
    low = value - high - middle
    info = jnp.zeros((INFO, BD), F32)
    for j, part in enumerate((rows.astype(F32), cols.astype(F32), high, middle, low)):
        info = jnp.where(row == j, part, info)
    return block.astype(BF), info.astype(BF)


def first_kernel(dims_in, energy_in, wave_in, out, dims, energy, wave, sems):
    b = color_of(lax.axis_index("op")) ^ 3
    copies = [
        pltpu.make_async_copy(dims_in, dims, sems.at[0]),
        pltpu.make_async_copy(energy_in, energy, sems.at[1]),
        pltpu.make_async_copy(wave_in.at[b], wave, sems.at[2]),
    ]
    for copy in copies:
        copy.start()
    for copy in copies:
        copy.wait()
    out[:BD], out[BD:] = pack(dims[0, b], dims[1, b], energy[b], wave[...])


def load_kernel(
    first, dims_in, energy_in, wave_in, left, right,
    own, left_out, right_out, token, dims, energy, wave, sems,
):
    copies = [
        pltpu.make_async_copy(dims_in, dims, sems.at[0]),
        pltpu.make_async_copy(energy_in, energy, sems.at[1]),
        pltpu.make_async_copy(wave_in, wave, sems.at[2]),
        pltpu.make_async_copy(left, left_out, sems.at[3]),
        pltpu.make_async_copy(right.at[pl.ds(0, HALF)], right_out, sems.at[4]),
    ]
    for copy in copies:
        copy.start()
    token[...] = jnp.zeros_like(token)
    for copy in copies[:3]:
        copy.wait()
    for b in range(4):
        own[b, :BD], own[b, BD:] = pack(dims[0, b], dims[1, b], energy[b], wave[b])
    for copy in copies[3:]:
        copy.wait()


def slot_terms(src, vec, left, right, e, first):
    inner = [
        jnp.dot(left[first + t, e], vec[src[e, first + t]], preferred_element_type=F32).astype(BF)
        for t in range(HALF)
    ]
    return lax.dot_general(
        jnp.concatenate(inner, axis=1),
        jnp.concatenate([right[t, e] for t in range(HALF)], axis=1),
        (((1,), (1,)), ((), ())),
        preferred_element_type=F32,
    )


def wave_kernel(
    src_in, own, core, far0, far1, far2, far3, near0, near1, near2, near3,
    left, right_a, right_in, token, out, vec, info, squares, right_b, src, acc, src_sem, sem,
):
    src_copy = pltpu.make_async_copy(src_in, src, src_sem)
    src_copy.start()
    right_copy = pltpu.make_async_copy(right_in.at[pl.ds(HALF, HALF)], right_b, sem)
    right_copy.start()
    me, color = lax.axis_index("blk"), color_of(lax.axis_index("op"))
    blocks = []
    for b in range(4):
        blocks.append((me * 4 + b, own.at[b]))
        blocks.append(((me ^ 1) * 4 + b, core.at[b]))
    for flip, pieces in ((2, (far0, far1, far2, far3)), (3, (near0, near1, near2, near3))):
        for b, piece in enumerate(pieces):
            blocks.append(((me ^ flip) * 4 + (color ^ b), piece))
    for block, piece in blocks:
        vec[block] = piece[:BD]
        entry = piece[BD:].astype(F32)
        info[block, 0:2] = entry[0:2]
        info[block, 2:3] = entry[2:3] + entry[3:4] + entry[4:5]
    src_copy.wait()
    plain, weighted = jnp.zeros((8, BD), F32), jnp.zeros((8, BD), F32)
    for e in range(4):
        acc[e] = slot_terms(src, vec, left, right_a, e, 0)
        for block in range(e * 4, e * 4 + 4):
            part = jnp.zeros((8, BD), F32)
            for r in range(0, BD, STRIP):
                vector = vec[block, r:r + STRIP].astype(F32)
                part += fold(vector * vector)
            plain += part
            weighted += info[block, 2:3] * part
    squares[0], squares[1] = plain, weighted
    right_copy.wait()
    for e in range(4):
        out[e] = (acc[e] + slot_terms(src, vec, left, right_b, e, HALF)).astype(BF)


def total_of(x):
    return jnp.sum(jnp.sum(x, axis=1, keepdims=True), axis=0, keepdims=True)


def fold(x):
    return jnp.sum(x.reshape(STRIP // 8, 8, BD), axis=0)


def corr_kernel(
    src, wave, info, squares, same, other, left, right_a, right_b,
    applied_out, corr_out, out, vec, acc, work, applied, applied_sem,
):
    entries = 16 * BD * BD
    me = lax.axis_index("blk")
    zero = jnp.zeros((8, BD), F32)
    strips = [pl.ds(r, STRIP) for r in range(0, BD, STRIP)]

    def summed(group, turn):
        b = me ^ turn
        return b, (same if turn % 2 == 0 else other).at[b >> 1, group]

    def cross_sums(group, cross):
        for turn in range(4):
            b, values = summed(group, turn)
            for rows in strips:
                cross += fold(values[rows].astype(F32) * wave[group * 4 + b, rows].astype(F32))
        return cross

    square = squares[0]
    cross = lax.fori_loop(0, 4, cross_sums, squares[1])
    rayleigh = total_of(cross) / entries / (total_of(square) / entries + 1e-06)

    def subtract(group, resid):
        for turn in range(4):
            b, values = summed(group, turn)
            block = group * 4 + b
            level = info[block, 2:3] - rayleigh
            for rows in strips:
                rest = values[rows].astype(F32) + level * wave[block, rows].astype(F32)
                work[block, rows] = rest
                resid += fold(rest * rest)
        return resid

    resid = lax.fori_loop(0, 4, subtract, zero)
    scale = lax.rsqrt(total_of(resid) / entries + 1e-06)
    for turn in range(4):
        b, values = summed(me, turn)
        level = info[me * 4 + b, 2:3]
        for rows in strips:
            vector = wave[me * 4 + b, rows].astype(F32)
            applied[b, rows] = values[rows].astype(F32) + level * vector

    applied_copy = pltpu.make_async_copy(applied, applied_out, applied_sem)
    applied_copy.start()

    @pl.loop(0, 4)
    def _(group):
        for b in range(4):
            for rows in strips:
                vec[group * 4 + b, rows] = (work[group * 4 + b, rows] * scale).astype(BF)

    for b in range(4):
        corr_out[b] = vec[me * 4 + b]

    for e in range(4):
        acc[e] = slot_terms(src, vec, left, right_a, e, 0)
    for e in range(4):
        total = acc[e] + slot_terms(src, vec, left, right_b, e, HALF)
        for i in range(16):
            for j in range(2):
                tile = total[i * 16:(i + 1) * 16, j * 128:(j + 1) * 128]
                out[i * 2 + j, e] = tile.astype(BF)
    applied_copy.wait()


def sum_wave_kernel(info, parts, out):
    part = lax.axis_index("op")
    entry = info[(part >> 3) * 4 + lax.axis_index("blk")]
    mask = live(entry[0:1], entry[1:2], (STRIP, BD), (part & 7) * STRIP)
    total = jnp.sum(parts[...].astype(F32), axis=0)
    total = jnp.where(mask, total, 0.0).astype(BF)
    for i in range(out.shape[0]):
        out[i] = total


def sum_corr_kernel(info, parts, out):
    part = lax.axis_index("op")
    totals = []
    for b in range(4):
        entry = info[lax.axis_index("blk") * 4 + b][:, :128]
        total = jnp.sum(parts[:, b].astype(F32), axis=0)
        mask = live(entry[0:1], entry[1:2], (16, 128), (part >> 1) * 16, (part & 1) * 128)
        totals.append(jnp.where(mask, total, 0.0).astype(BF))
    for i in range(out.shape[0]):
        for b in range(4):
            out[i, b] = totals[b]


def final_kernel(info, parts, corr, out, blocks, sems):
    copies = []
    for b in range(4):
        level = info[lax.axis_index("blk") * 4 + b, 2:3]
        for i in range(16):
            rows = pl.ds(i * 16, 16)
            summed = jnp.concatenate([parts[2 * i, b], parts[2 * i + 1, b]], axis=1)
            blocks[b, rows] = summed.astype(F32) + level * corr[b, rows].astype(F32)
        copies.append(pltpu.make_async_copy(blocks.at[b], out.at[b], sems.at[b]))
        copies[b].start()
    for copy in copies:
        copy.wait()


def params(mib):
    return pltpu.CompilerParams(vmem_limit_bytes=mib * MIB)


def shape(dims, kind=BF):
    return jax.ShapeDtypeStruct(dims, kind)


def shards(wave_blocks, left_env, right_env, source, block_dims, energy):
    src = source.T

    dims_in, energy_in, wave_in, left_in, right_in = (
        pltpu.with_memory_space_constraint(x, pltpu.HBM)
        for x in (block_dims, energy, wave_blocks, left_env, right_env)
    )
    half = (HALF,) + right_env.shape[1:]
    small = [pltpu.SMEM((2, 4), jnp.int32), pltpu.SMEM((4,), F32)]
    first = pl.pallas_call(
        first_kernel,
        out_shape=shape((ROWS, BD)),
        in_specs=[HBM] * 3,
        out_specs=VMEM,
        scratch_shapes=small + [pltpu.VMEM((BD, BD), BF), pltpu.SemaphoreType.DMA((3,))],
        compiler_params=params(2),
        name="pack_first",
    )(dims_in, energy_in, wave_in)
    far = [lax.ppermute(first, ALL, cross_pairs())]
    own, left, right_a, token = pl.pallas_call(
        load_kernel,
        out_shape=(
            shape((4, ROWS, BD)), pltpu.VMEM(left_env.shape, BF), pltpu.VMEM(half, BF),
            shape((8, 128), F32),
        ),
        in_specs=[VMEM] + [HBM] * 5,
        out_specs=(VMEM,) * 4,
        scratch_shapes=small + [pltpu.VMEM((4, BD, BD), BF), pltpu.SemaphoreType.DMA((5,))],
        compiler_params=params(4),
        name="load",
    )(first, dims_in, energy_in, wave_in, left_in, right_in)
    far[0], own, token = lax.optimization_barrier((far[0], own, token))
    core = lax.ppermute(own, "blk", core_pairs())
    for bit in (1, 4, 16):
        far.append(lax.ppermute(far[0], "op", flip_pairs(bit)))
    near = [lax.ppermute(piece, "blk", core_pairs()) for piece in far]

    partial, wave, info, squares, right_b = pl.pallas_call(
        wave_kernel,
        out_shape=(
            shape((4, BD, BD)), shape((16, BD, BD)), shape((16, 8, BD), F32),
            shape((2, 8, BD), F32), pltpu.VMEM(half, BF),
        ),
        in_specs=[HBM] + [VMEM] * 12 + [HBM, VMEM],
        out_specs=(VMEM,) * 5,
        scratch_shapes=[
            pltpu.SMEM((4, 16), jnp.int32),
            pltpu.VMEM((4, BD, BD), F32),
            pltpu.SemaphoreType.DMA,
            pltpu.SemaphoreType.DMA,
        ],
        compiler_params=params(8),
        name="wave_terms",
    )(
        pltpu.with_memory_space_constraint(src, pltpu.HBM), own, core, *far, *near,
        left, right_a, right_in, token,
    )

    pieces = lax.all_to_all(partial.reshape(32, 32, BD), "op", 0, 0, tiled=True)
    copies = pl.pallas_call(
        sum_wave_kernel,
        out_shape=shape((64, 32, BD)),
        in_specs=[VMEM, VMEM],
        out_specs=VMEM,
        compiler_params=params(8),
        name="sum_wave",
    )(info, pieces)
    same = lax.all_to_all(
        copies, ALL, 0, 0, tiled=True, axis_index_groups=core_groups()
    )
    other = lax.ppermute(same, "blk", core_pairs())

    applied_wave, corr, partial = pl.pallas_call(
        corr_kernel,
        out_shape=(shape((4, BD, BD), F32), shape((4, BD, BD)), shape((32, 4, 16, 128))),
        in_specs=[SMEM] + [VMEM] * 8,
        out_specs=(HBM, VMEM, VMEM),
        scratch_shapes=[
            pltpu.VMEM((16, BD, BD), BF),
            pltpu.VMEM((4, BD, BD), F32),
            pltpu.VMEM((16, BD, BD), F32),
            pltpu.VMEM((4, BD, BD), F32),
            pltpu.SemaphoreType.DMA,
        ],
        compiler_params=params(14),
        name="corr_terms",
    )(
        src, wave, info, squares,
        same.reshape(2, 4, BD, BD), other.reshape(2, 4, BD, BD), left, right_a, right_b,
    )

    pieces = lax.all_to_all(partial.reshape(128, 16, 128), ALL, 0, 0, tiled=True)
    copies = pl.pallas_call(
        sum_corr_kernel,
        out_shape=shape((32, 4, 16, 128)),
        in_specs=[VMEM, VMEM],
        out_specs=VMEM,
        compiler_params=params(8),
        name="sum_corr",
    )(info, pieces.reshape(32, 4, 16, 128))
    gathered = lax.all_to_all(copies, "op", 0, 0, tiled=True)
    applied_corr = pl.pallas_call(
        final_kernel,
        out_shape=shape((4, BD, BD), F32),
        in_specs=[VMEM, VMEM, VMEM],
        out_specs=HBM,
        scratch_shapes=[pltpu.VMEM((4, BD, BD), F32), pltpu.SemaphoreType.DMA((4,))],
        compiler_params=params(8),
        name="finish",
    )(info, gathered, corr)
    return (applied_wave, applied_corr)


def solution(mesh):
    placed = (
        P("blk", None, None),
        P("op", "blk", None, None),
        P("op", "blk", None, None),
        P("op", "blk"),
        P(None, "blk"),
        P("blk"),
    )
    return jax.shard_map(
        shards,
        mesh=mesh,
        in_specs=placed,
        out_specs=(P("blk", None, None), P("blk", None, None)),
        check_vma=False,
    )
```

```python
import jax
import jax.numpy as jnp
from jax import lax
from jax.experimental import pallas as pl
from jax.experimental.pallas import tpu as pltpu
from jax.sharding import PartitionSpec as P

BF = jnp.bfloat16
F32 = jnp.float32
BD = 256
INFO = 16
ROWS = BD + INFO
HALF = 8
STRIP = 32
MIB = 1 << 20
UNIT = 2.0 ** 20
SLOPE = 5.8
LN2 = 0.6931471805599453
ALL = ("op", "blk")

SMEM = pl.BlockSpec(memory_space=pltpu.SMEM)
VMEM = pl.BlockSpec(memory_space=pltpu.VMEM)
HBM = pl.BlockSpec(memory_space=pltpu.HBM)


def device(op, blk):
    return op * 4 + blk


def cross_pairs():
    return [(device(o, b), device(o ^ 16, b ^ 2)) for o in range(32) for b in range(4)]


def flip_pairs(bit):
    return [(o, o ^ bit) for o in range(32)]


def color_of(op):
    x, y, z = op & 1, (op >> 2) & 1, op >> 4
    return (x ^ z) + 2 * (y ^ z)


def core_pairs():
    return [(b, b ^ 1) for b in range(4)]


def core_groups():
    return [[device(o, zh * 2 + c) for zh in range(2) for o in range(32)] for c in range(2)]


def live(rows, cols, shape, first_row=0, first_col=0):
    row_ids = lax.broadcasted_iota(jnp.int32, shape, 0) + first_row
    col_ids = lax.broadcasted_iota(jnp.int32, shape, 1) + first_col
    return (row_ids < rows) & (col_ids < cols)


def pack(rows, cols, energy, wave):
    row = lax.broadcasted_iota(jnp.int32, (INFO, BD), 0)
    block = jnp.where(live(rows, cols, (BD, BD)), wave.astype(F32), 0.0)
    value = jnp.full((INFO, BD), energy, F32)
    high = value.astype(BF).astype(F32)
    middle = (value - high).astype(BF).astype(F32)
    low = value - high - middle
    info = jnp.zeros((INFO, BD), F32)
    for j, part in enumerate((rows.astype(F32), cols.astype(F32), high, middle, low)):
        info = jnp.where(row == j, part, info)
    return block.astype(BF), info.astype(BF)


def first_kernel(dims_in, energy_in, wave_in, out, dims, energy, wave, sems):
    b = color_of(lax.axis_index("op")) ^ 3
    copies = [
        pltpu.make_async_copy(dims_in, dims, sems.at[0]),
        pltpu.make_async_copy(energy_in, energy, sems.at[1]),
        pltpu.make_async_copy(wave_in.at[b], wave, sems.at[2]),
    ]
    for copy in copies:
        copy.start()
    for copy in copies:
        copy.wait()
    out[:BD], out[BD:] = pack(dims[0, b], dims[1, b], energy[b], wave[...])


def load_kernel(
    first, dims_in, energy_in, wave_in, left, right,
    own, left_out, right_out, token, dims, energy, wave, sems,
):
    copies = [
        pltpu.make_async_copy(dims_in, dims, sems.at[0]),
        pltpu.make_async_copy(energy_in, energy, sems.at[1]),
        pltpu.make_async_copy(wave_in, wave, sems.at[2]),
        pltpu.make_async_copy(left, left_out, sems.at[3]),
        pltpu.make_async_copy(right.at[pl.ds(0, HALF)], right_out, sems.at[4]),
    ]
    for copy in copies:
        copy.start()
    token[...] = jnp.zeros_like(token)
    for copy in copies[:3]:
        copy.wait()
    for b in range(4):
        own[b, :BD], own[b, BD:] = pack(dims[0, b], dims[1, b], energy[b], wave[b])
    for copy in copies[3:]:
        copy.wait()


def slot_terms(src, vec, left, right, e, first):
    inner = [
        jnp.dot(left[first + t, e], vec[src[e, first + t]], preferred_element_type=F32).astype(BF)
        for t in range(HALF)
    ]
    return lax.dot_general(
        jnp.concatenate(inner, axis=1),
        jnp.concatenate([right[t, e] for t in range(HALF)], axis=1),
        (((1,), (1,)), ((), ())),
        preferred_element_type=F32,
    )


def wave_kernel(
    src_in, own, core, far0, far1, far2, far3, near0, near1, near2, near3,
    left, right_a, right_in, token, out, vec, info, squares, right_b, src, acc, src_sem, sem,
):
    src_copy = pltpu.make_async_copy(src_in, src, src_sem)
    src_copy.start()
    right_copy = pltpu.make_async_copy(right_in.at[pl.ds(HALF, HALF)], right_b, sem)
    right_copy.start()
    me, color = lax.axis_index("blk"), color_of(lax.axis_index("op"))
    blocks = []
    for b in range(4):
        blocks.append((me * 4 + b, own.at[b]))
        blocks.append(((me ^ 1) * 4 + b, core.at[b]))
    for flip, pieces in ((2, (far0, far1, far2, far3)), (3, (near0, near1, near2, near3))):
        for b, piece in enumerate(pieces):
            blocks.append(((me ^ flip) * 4 + (color ^ b), piece))
    for block, piece in blocks:
        vec[block] = piece[:BD]
        entry = piece[BD:].astype(F32)
        info[block, 0:2] = entry[0:2]
        info[block, 2:3] = entry[2:3] + entry[3:4] + entry[4:5]
    src_copy.wait()
    plain, weighted = jnp.zeros((8, BD), F32), jnp.zeros((8, BD), F32)
    for e in range(4):
        acc[e] = slot_terms(src, vec, left, right_a, e, 0)
        for block in range(e * 4, e * 4 + 4):
            part = jnp.zeros((8, BD), F32)
            for r in range(0, BD, STRIP):
                vector = vec[block, r:r + STRIP].astype(F32)
                part += fold(vector * vector)
            plain += part
            weighted += info[block, 2:3] * part
    squares[0], squares[1] = plain, weighted
    right_copy.wait()
    for e in range(4):
        out[e] = encode(acc[e] + slot_terms(src, vec, left, right_b, e, HALF))


def encode(x):
    level = jnp.log(1.0 + jnp.abs(x) * UNIT) * (SLOPE / LN2)
    size = jnp.exp2(level - 120.0)
    return jnp.where(x < 0.0, -size, size).astype(BF)


def decode(code):
    code = code.astype(F32)
    size = jnp.abs(code)
    level = (jnp.log(size) * (1.0 / LN2) + 120.0) * (1.0 / SLOPE)
    value = jnp.where(size > 2.0 ** -120, (jnp.exp2(level) - 1.0) * (1.0 / UNIT), 0.0)
    return jnp.where(code < 0.0, -value, value)


def total_of(x):
    return jnp.sum(jnp.sum(x, axis=1, keepdims=True), axis=0, keepdims=True)


def fold(x):
    return jnp.sum(x.reshape(STRIP // 8, 8, BD), axis=0)


def corr_kernel(
    src, wave, info, squares, same, other, left, right_a, right_b,
    applied_out, corr_out, out, vec, acc, work, applied, applied_sem,
):
    entries = 16 * BD * BD
    me = lax.axis_index("blk")
    zero = jnp.zeros((8, BD), F32)
    strips = [pl.ds(r, STRIP) for r in range(0, BD, STRIP)]

    def summed(group, turn):
        b = me ^ turn
        return b, (same if turn % 2 == 0 else other).at[b >> 1, group]

    def cross_sums(group, cross):
        for turn in range(4):
            b, values = summed(group, turn)
            for rows in strips:
                value = decode(values[rows])
                work[group * 4 + b, rows] = value
                cross += fold(value * wave[group * 4 + b, rows].astype(F32))
        return cross

    square = squares[0]
    cross = lax.fori_loop(0, 4, cross_sums, squares[1])
    rayleigh = total_of(cross) / entries / (total_of(square) / entries + 1e-06)

    def subtract(group, resid):
        for b in range(4):
            block = group * 4 + b
            level = info[block, 2:3] - rayleigh
            for rows in strips:
                rest = work[block, rows] + level * wave[block, rows].astype(F32)
                work[block, rows] = rest
                resid += fold(rest * rest)
        return resid

    resid = lax.fori_loop(0, 4, subtract, zero)
    scale = lax.rsqrt(total_of(resid) / entries + 1e-06)
    for b in range(4):
        for rows in strips:
            applied[b, rows] = work[me * 4 + b, rows] + rayleigh * wave[me * 4 + b, rows].astype(F32)

    applied_copy = pltpu.make_async_copy(applied, applied_out, applied_sem)
    applied_copy.start()

    @pl.loop(0, 4)
    def _(group):
        for b in range(4):
            for rows in strips:
                vec[group * 4 + b, rows] = (work[group * 4 + b, rows] * scale).astype(BF)

    for b in range(4):
        corr_out[b] = vec[me * 4 + b]

    for e in range(4):
        acc[e] = slot_terms(src, vec, left, right_a, e, 0)
    for e in range(4):
        total = acc[e] + slot_terms(src, vec, left, right_b, e, HALF)
        for i in range(16):
            for j in range(2):
                tile = total[i * 16:(i + 1) * 16, j * 128:(j + 1) * 128]
                out[i * 2 + j, e] = tile.astype(BF)
    applied_copy.wait()


def sum_wave_kernel(info, parts, out):
    part = lax.axis_index("op")
    entry = info[(part >> 3) * 4 + lax.axis_index("blk")]
    mask = live(entry[0:1], entry[1:2], (STRIP, BD), (part & 7) * STRIP)
    total = jnp.zeros((STRIP, BD), F32)
    for i in range(parts.shape[0]):
        total += decode(parts[i])
    total = encode(jnp.where(mask, total, 0.0))
    for i in range(out.shape[0]):
        out[i] = total


def sum_corr_kernel(info, parts, out):
    part = lax.axis_index("op")
    totals = []
    for b in range(4):
        entry = info[lax.axis_index("blk") * 4 + b][:, :128]
        total = jnp.sum(parts[:, b].astype(F32), axis=0)
        mask = live(entry[0:1], entry[1:2], (16, 128), (part >> 1) * 16, (part & 1) * 128)
        totals.append(jnp.where(mask, total, 0.0).astype(BF))
    for i in range(out.shape[0]):
        for b in range(4):
            out[i, b] = totals[b]


def final_kernel(info, parts, corr, out, blocks, sems):
    copies = []
    for b in range(4):
        level = info[lax.axis_index("blk") * 4 + b, 2:3]
        for i in range(16):
            rows = pl.ds(i * 16, 16)
            summed = jnp.concatenate([parts[2 * i, b], parts[2 * i + 1, b]], axis=1)
            blocks[b, rows] = summed.astype(F32) + level * corr[b, rows].astype(F32)
        copies.append(pltpu.make_async_copy(blocks.at[b], out.at[b], sems.at[b]))
        copies[b].start()
    for copy in copies:
        copy.wait()


def params(mib):
    return pltpu.CompilerParams(vmem_limit_bytes=mib * MIB)


def shape(dims, kind=BF):
    return jax.ShapeDtypeStruct(dims, kind)


def shards(wave_blocks, left_env, right_env, source, block_dims, energy):
    src = source.T

    dims_in, energy_in, wave_in, left_in, right_in = (
        pltpu.with_memory_space_constraint(x, pltpu.HBM)
        for x in (block_dims, energy, wave_blocks, left_env, right_env)
    )
    half = (HALF,) + right_env.shape[1:]
    small = [pltpu.SMEM((2, 4), jnp.int32), pltpu.SMEM((4,), F32)]
    first = pl.pallas_call(
        first_kernel,
        out_shape=shape((ROWS, BD)),
        in_specs=[HBM] * 3,
        out_specs=VMEM,
        scratch_shapes=small + [pltpu.VMEM((BD, BD), BF), pltpu.SemaphoreType.DMA((3,))],
        compiler_params=params(2),
        name="pack_first",
    )(dims_in, energy_in, wave_in)
    far = [lax.ppermute(first, ALL, cross_pairs())]
    own, left, right_a, token = pl.pallas_call(
        load_kernel,
        out_shape=(
            shape((4, ROWS, BD)), pltpu.VMEM(left_env.shape, BF), pltpu.VMEM(half, BF),
            shape((8, 128), F32),
        ),
        in_specs=[VMEM] + [HBM] * 5,
        out_specs=(VMEM,) * 4,
        scratch_shapes=small + [pltpu.VMEM((4, BD, BD), BF), pltpu.SemaphoreType.DMA((5,))],
        compiler_params=params(4),
        name="load",
    )(first, dims_in, energy_in, wave_in, left_in, right_in)
    far[0], own, token = lax.optimization_barrier((far[0], own, token))
    core = lax.ppermute(own, "blk", core_pairs())
    for bit in (1, 4, 16):
        far.append(lax.ppermute(far[0], "op", flip_pairs(bit)))
    near = [lax.ppermute(piece, "blk", core_pairs()) for piece in far]

    partial, wave, info, squares, right_b = pl.pallas_call(
        wave_kernel,
        out_shape=(
            shape((4, BD, BD)), shape((16, BD, BD)), shape((16, 8, BD), F32),
            shape((2, 8, BD), F32), pltpu.VMEM(half, BF),
        ),
        in_specs=[HBM] + [VMEM] * 12 + [HBM, VMEM],
        out_specs=(VMEM,) * 5,
        scratch_shapes=[
            pltpu.SMEM((4, 16), jnp.int32),
            pltpu.VMEM((4, BD, BD), F32),
            pltpu.SemaphoreType.DMA,
            pltpu.SemaphoreType.DMA,
        ],
        compiler_params=params(8),
        name="wave_terms",
    )(
        pltpu.with_memory_space_constraint(src, pltpu.HBM), own, core, *far, *near,
        left, right_a, right_in, token,
    )

    pieces = lax.all_to_all(partial.reshape(32, 32, BD), "op", 0, 0, tiled=True)
    copies = pl.pallas_call(
        sum_wave_kernel,
        out_shape=shape((64, 32, BD)),
        in_specs=[VMEM, VMEM],
        out_specs=VMEM,
        compiler_params=params(8),
        name="sum_wave",
    )(info, pieces)
    same = lax.all_to_all(
        copies, ALL, 0, 0, tiled=True, axis_index_groups=core_groups()
    )
    other = lax.ppermute(same, "blk", core_pairs())

    applied_wave, corr, partial = pl.pallas_call(
        corr_kernel,
        out_shape=(shape((4, BD, BD), F32), shape((4, BD, BD)), shape((32, 4, 16, 128))),
        in_specs=[SMEM] + [VMEM] * 8,
        out_specs=(HBM, VMEM, VMEM),
        scratch_shapes=[
            pltpu.VMEM((16, BD, BD), BF),
            pltpu.VMEM((4, BD, BD), F32),
            pltpu.VMEM((16, BD, BD), F32),
            pltpu.VMEM((4, BD, BD), F32),
            pltpu.SemaphoreType.DMA,
        ],
        compiler_params=params(14),
        name="corr_terms",
    )(
        src, wave, info, squares,
        same.reshape(2, 4, BD, BD), other.reshape(2, 4, BD, BD), left, right_a, right_b,
    )

    pieces = lax.all_to_all(partial.reshape(128, 16, 128), ALL, 0, 0, tiled=True)
    copies = pl.pallas_call(
        sum_corr_kernel,
        out_shape=shape((32, 4, 16, 128)),
        in_specs=[VMEM, VMEM],
        out_specs=VMEM,
        compiler_params=params(8),
        name="sum_corr",
    )(info, pieces.reshape(32, 4, 16, 128))
    gathered = lax.all_to_all(copies, "op", 0, 0, tiled=True)
    applied_corr = pl.pallas_call(
        final_kernel,
        out_shape=shape((4, BD, BD), F32),
        in_specs=[VMEM, VMEM, VMEM],
        out_specs=HBM,
        scratch_shapes=[pltpu.VMEM((4, BD, BD), F32), pltpu.SemaphoreType.DMA((4,))],
        compiler_params=params(8),
        name="finish",
    )(info, gathered, corr)
    return (applied_wave, applied_corr)


def solution(mesh):
    placed = (
        P("blk", None, None),
        P("op", "blk", None, None),
        P("op", "blk", None, None),
        P("op", "blk"),
        P(None, "blk"),
        P("blk"),
    )
    return jax.shard_map(
        shards,
        mesh=mesh,
        in_specs=placed,
        out_specs=(P("blk", None, None), P("blk", None, None)),
        check_vma=False,
    )
```

```python
import jax
import jax.numpy as jnp
from jax import lax
from jax.experimental import pallas as pl
from jax.experimental.pallas import tpu as pltpu
from jax.sharding import PartitionSpec as P

BF = jnp.bfloat16
F32 = jnp.float32
BD = 256
INFO = 16
ROWS = BD + INFO
HALF = 8
STRIP = 32
MIB = 1 << 20
UNIT = 2.0 ** 20
SLOPE = 5.8
LN2 = 0.6931471805599453
ALL = ("op", "blk")

SMEM = pl.BlockSpec(memory_space=pltpu.SMEM)
VMEM = pl.BlockSpec(memory_space=pltpu.VMEM)
HBM = pl.BlockSpec(memory_space=pltpu.HBM)


def device(op, blk):
    return op * 4 + blk


def cross_pairs():
    return [(device(o, b), device(o ^ 16, b ^ 2)) for o in range(32) for b in range(4)]


def flip_pairs(bit):
    return [(o, o ^ bit) for o in range(32)]


def color_of(op):
    x, y, z = op & 1, (op >> 2) & 1, op >> 4
    return (x ^ z) + 2 * (y ^ z)


def core_pairs():
    return [(b, b ^ 1) for b in range(4)]


def core_groups():
    return [[device(o, zh * 2 + c) for zh in range(2) for o in range(32)] for c in range(2)]


def live(rows, cols, shape, first_row=0, first_col=0):
    row_ids = lax.broadcasted_iota(jnp.int32, shape, 0) + first_row
    col_ids = lax.broadcasted_iota(jnp.int32, shape, 1) + first_col
    return (row_ids < rows) & (col_ids < cols)


def pack(rows, cols, energy, wave):
    row = lax.broadcasted_iota(jnp.int32, (INFO, BD), 0)
    block = jnp.where(live(rows, cols, (BD, BD)), wave.astype(F32), 0.0)
    value = jnp.full((INFO, BD), energy, F32)
    high = value.astype(BF).astype(F32)
    middle = (value - high).astype(BF).astype(F32)
    low = value - high - middle
    info = jnp.zeros((INFO, BD), F32)
    for j, part in enumerate((rows.astype(F32), cols.astype(F32), high, middle, low)):
        info = jnp.where(row == j, part, info)
    return block.astype(BF), info.astype(BF)


def first_kernel(dims_in, energy_in, wave_in, out, dims, energy, wave, sems):
    b = color_of(lax.axis_index("op")) ^ 3
    copies = [
        pltpu.make_async_copy(dims_in, dims, sems.at[0]),
        pltpu.make_async_copy(energy_in, energy, sems.at[1]),
        pltpu.make_async_copy(wave_in.at[b], wave, sems.at[2]),
    ]
    for copy in copies:
        copy.start()
    for copy in copies:
        copy.wait()
    out[:BD], out[BD:] = pack(dims[0, b], dims[1, b], energy[b], wave[...])


def load_kernel(
    first, dims_in, energy_in, wave_in, left, right,
    own, left_out, right_out, token, dims, energy, wave, sems,
):
    copies = [
        pltpu.make_async_copy(dims_in, dims, sems.at[0]),
        pltpu.make_async_copy(energy_in, energy, sems.at[1]),
        pltpu.make_async_copy(wave_in, wave, sems.at[2]),
        pltpu.make_async_copy(left, left_out, sems.at[3]),
        pltpu.make_async_copy(right.at[pl.ds(0, HALF)], right_out, sems.at[4]),
    ]
    for copy in copies:
        copy.start()
    token[...] = jnp.zeros_like(token)
    for copy in copies[:3]:
        copy.wait()
    for b in range(4):
        own[b, :BD], own[b, BD:] = pack(dims[0, b], dims[1, b], energy[b], wave[b])
    for copy in copies[3:]:
        copy.wait()


def slot_terms(src, vec, left, right, e, first):
    inner = [
        jnp.dot(left[first + t, e], vec[src[e, first + t]], preferred_element_type=F32).astype(BF)
        for t in range(HALF)
    ]
    return lax.dot_general(
        jnp.concatenate(inner, axis=1),
        jnp.concatenate([right[t, e] for t in range(HALF)], axis=1),
        (((1,), (1,)), ((), ())),
        preferred_element_type=F32,
    )


def wave_kernel(
    src_in, own, core, far0, far1, far2, far3, near0, near1, near2, near3,
    left, right_a, right_in, token, out, vec, info, squares, right_b, src, acc, src_sem, sem,
):
    src_copy = pltpu.make_async_copy(src_in, src, src_sem)
    src_copy.start()
    right_copy = pltpu.make_async_copy(right_in.at[pl.ds(HALF, HALF)], right_b, sem)
    right_copy.start()
    me, color = lax.axis_index("blk"), color_of(lax.axis_index("op"))
    blocks = []
    for b in range(4):
        blocks.append((me * 4 + b, own.at[b]))
        blocks.append(((me ^ 1) * 4 + b, core.at[b]))
    for flip, pieces in ((2, (far0, far1, far2, far3)), (3, (near0, near1, near2, near3))):
        for b, piece in enumerate(pieces):
            blocks.append(((me ^ flip) * 4 + (color ^ b), piece))
    for block, piece in blocks:
        vec[block] = piece[:BD]
        entry = piece[BD:].astype(F32)
        info[block, 0:2] = entry[0:2]
        info[block, 2:3] = entry[2:3] + entry[3:4] + entry[4:5]
    src_copy.wait()
    plain, weighted = jnp.zeros((8, BD), F32), jnp.zeros((8, BD), F32)
    for e in range(4):
        acc[e] = slot_terms(src, vec, left, right_a, e, 0)
        for block in range(e * 4, e * 4 + 4):
            part = jnp.zeros((8, BD), F32)
            for r in range(0, BD, STRIP):
                vector = vec[block, r:r + STRIP].astype(F32)
                part += fold(vector * vector)
            plain += part
            weighted += info[block, 2:3] * part
    squares[0], squares[1] = plain, weighted
    right_copy.wait()
    for e in range(4):
        out[e] = encode(acc[e] + slot_terms(src, vec, left, right_b, e, HALF))


def encode(x):
    level = jnp.log(1.0 + jnp.abs(x) * UNIT) * (SLOPE / LN2)
    size = jnp.exp2(level - 120.0)
    return jnp.where(x < 0.0, -size, size).astype(BF)


def decode(code):
    code = code.astype(F32)
    size = jnp.abs(code)
    level = (jnp.log(size) * (1.0 / LN2) + 120.0) * (1.0 / SLOPE)
    value = jnp.where(size > 2.0 ** -120, (jnp.exp2(level) - 1.0) * (1.0 / UNIT), 0.0)
    return jnp.where(code < 0.0, -value, value)


def total_of(x):
    return jnp.sum(jnp.sum(x, axis=1, keepdims=True), axis=0, keepdims=True)


def fold(x):
    return jnp.sum(x.reshape(STRIP // 8, 8, BD), axis=0)


def decode_sums(work, codes, wave, me, turns, start):
    def add_group(group, cross):
        for turn in turns:
            b = me ^ turn
            for r in range(0, BD, STRIP):
                rows = pl.ds(r, STRIP)
                value = decode(codes[b >> 1, group, rows])
                work[group * 4 + b, rows] = value
                cross += fold(value * wave[group * 4 + b, rows].astype(F32))
        return cross

    return lax.fori_loop(0, 4, add_group, start)


def half_kernel(wave, squares, same, sums, work):
    sums[0] = squares[0]
    sums[1] = decode_sums(work, same, wave, lax.axis_index("blk"), (0, 2), squares[1])


def corr_kernel(
    src, wave, info, sums, work_in, other, left, right_a, right_b,
    applied_out, corr_out, out, work, vec, acc, applied, applied_sem,
):
    entries = 16 * BD * BD
    me = lax.axis_index("blk")
    zero = jnp.zeros((8, BD), F32)
    strips = [pl.ds(r, STRIP) for r in range(0, BD, STRIP)]

    square = sums[0]
    cross = decode_sums(work, other, wave, me, (1, 3), sums[1])
    rayleigh = total_of(cross) / entries / (total_of(square) / entries + 1e-06)

    def subtract(group, resid):
        for b in range(4):
            block = group * 4 + b
            level = info[block, 2:3] - rayleigh
            for rows in strips:
                rest = work[block, rows] + level * wave[block, rows].astype(F32)
                work[block, rows] = rest
                resid += fold(rest * rest)
        return resid

    resid = lax.fori_loop(0, 4, subtract, zero)
    scale = lax.rsqrt(total_of(resid) / entries + 1e-06)
    for b in range(4):
        for rows in strips:
            applied[b, rows] = work[me * 4 + b, rows] + rayleigh * wave[me * 4 + b, rows].astype(F32)

    applied_copy = pltpu.make_async_copy(applied, applied_out, applied_sem)
    applied_copy.start()

    @pl.loop(0, 4)
    def _(group):
        for b in range(4):
            for rows in strips:
                vec[group * 4 + b, rows] = (work[group * 4 + b, rows] * scale).astype(BF)

    for b in range(4):
        corr_out[b] = vec[me * 4 + b]

    for e in range(4):
        acc[e] = slot_terms(src, vec, left, right_a, e, 0)
    for e in range(4):
        total = acc[e] + slot_terms(src, vec, left, right_b, e, HALF)
        for i in range(16):
            for j in range(2):
                tile = total[i * 16:(i + 1) * 16, j * 128:(j + 1) * 128]
                out[i * 2 + j, e] = tile.astype(BF)
    applied_copy.wait()


def sum_wave_kernel(info, parts, out):
    part = lax.axis_index("op")
    entry = info[(part >> 3) * 4 + lax.axis_index("blk")]
    mask = live(entry[0:1], entry[1:2], (STRIP, BD), (part & 7) * STRIP)
    total = jnp.zeros((STRIP, BD), F32)
    for i in range(parts.shape[0]):
        total += decode(parts[i])
    total = encode(jnp.where(mask, total, 0.0))
    for i in range(out.shape[0]):
        out[i] = total


def sum_corr_kernel(info, parts, out):
    part = lax.axis_index("op")
    totals = []
    for b in range(4):
        entry = info[lax.axis_index("blk") * 4 + b][:, :128]
        total = jnp.sum(parts[:, b].astype(F32), axis=0)
        mask = live(entry[0:1], entry[1:2], (16, 128), (part >> 1) * 16, (part & 1) * 128)
        totals.append(jnp.where(mask, total, 0.0).astype(BF))
    for i in range(out.shape[0]):
        for b in range(4):
            out[i, b] = totals[b]


def final_kernel(info, parts, corr, out, blocks, sems):
    copies = []
    for b in range(4):
        level = info[lax.axis_index("blk") * 4 + b, 2:3]
        for i in range(16):
            rows = pl.ds(i * 16, 16)
            summed = jnp.concatenate([parts[2 * i, b], parts[2 * i + 1, b]], axis=1)
            blocks[b, rows] = summed.astype(F32) + level * corr[b, rows].astype(F32)
        copies.append(pltpu.make_async_copy(blocks.at[b], out.at[b], sems.at[b]))
        copies[b].start()
    for copy in copies:
        copy.wait()


def params(mib):
    return pltpu.CompilerParams(vmem_limit_bytes=mib * MIB)


def shape(dims, kind=BF):
    return jax.ShapeDtypeStruct(dims, kind)


def shards(wave_blocks, left_env, right_env, source, block_dims, energy):
    src = source.T

    dims_in, energy_in, wave_in, left_in, right_in = (
        pltpu.with_memory_space_constraint(x, pltpu.HBM)
        for x in (block_dims, energy, wave_blocks, left_env, right_env)
    )
    half = (HALF,) + right_env.shape[1:]
    small = [pltpu.SMEM((2, 4), jnp.int32), pltpu.SMEM((4,), F32)]
    first = pl.pallas_call(
        first_kernel,
        out_shape=shape((ROWS, BD)),
        in_specs=[HBM] * 3,
        out_specs=VMEM,
        scratch_shapes=small + [pltpu.VMEM((BD, BD), BF), pltpu.SemaphoreType.DMA((3,))],
        compiler_params=params(2),
        name="pack_first",
    )(dims_in, energy_in, wave_in)
    far = [lax.ppermute(first, ALL, cross_pairs())]
    own, left, right_a, token = pl.pallas_call(
        load_kernel,
        out_shape=(
            shape((4, ROWS, BD)), pltpu.VMEM(left_env.shape, BF), pltpu.VMEM(half, BF),
            shape((8, 128), F32),
        ),
        in_specs=[VMEM] + [HBM] * 5,
        out_specs=(VMEM,) * 4,
        scratch_shapes=small + [pltpu.VMEM((4, BD, BD), BF), pltpu.SemaphoreType.DMA((5,))],
        compiler_params=params(4),
        name="load",
    )(first, dims_in, energy_in, wave_in, left_in, right_in)
    far[0], own, token = lax.optimization_barrier((far[0], own, token))
    core = lax.ppermute(own, "blk", core_pairs())
    for bit in (1, 4, 16):
        far.append(lax.ppermute(far[0], "op", flip_pairs(bit)))
    near = [lax.ppermute(piece, "blk", core_pairs()) for piece in far]

    partial, wave, info, squares, right_b = pl.pallas_call(
        wave_kernel,
        out_shape=(
            shape((4, BD, BD)), shape((16, BD, BD)), shape((16, 8, BD), F32),
            shape((2, 8, BD), F32), pltpu.VMEM(half, BF),
        ),
        in_specs=[HBM] + [VMEM] * 12 + [HBM, VMEM],
        out_specs=(VMEM,) * 5,
        scratch_shapes=[
            pltpu.SMEM((4, 16), jnp.int32),
            pltpu.VMEM((4, BD, BD), F32),
            pltpu.SemaphoreType.DMA,
            pltpu.SemaphoreType.DMA,
        ],
        compiler_params=params(8),
        name="wave_terms",
    )(
        pltpu.with_memory_space_constraint(src, pltpu.HBM), own, core, *far, *near,
        left, right_a, right_in, token,
    )

    pieces = lax.all_to_all(partial.reshape(32, 32, BD), "op", 0, 0, tiled=True)
    copies = pl.pallas_call(
        sum_wave_kernel,
        out_shape=shape((64, 32, BD)),
        in_specs=[VMEM, VMEM],
        out_specs=VMEM,
        compiler_params=params(8),
        name="sum_wave",
    )(info, pieces)
    same = lax.all_to_all(
        copies, ALL, 0, 0, tiled=True, axis_index_groups=core_groups()
    )
    other = lax.ppermute(same, "blk", core_pairs())
    sums, work = pl.pallas_call(
        half_kernel,
        out_shape=(shape((2, 8, BD), F32), shape((16, BD, BD), F32)),
        in_specs=[VMEM] * 3,
        out_specs=(VMEM, VMEM),
        compiler_params=params(2),
        cost_estimate=pl.CostEstimate(
            flops=16 * MIB, bytes_accessed=4 * MIB, transcendentals=MIB
        ),
        name="decode_half",
    )(wave, squares, same.reshape(2, 4, BD, BD))

    applied_wave, corr, partial, work = pl.pallas_call(
        corr_kernel,
        out_shape=(
            shape((4, BD, BD), F32), shape((4, BD, BD)), shape((32, 4, 16, 128)),
            shape((16, BD, BD), F32),
        ),
        in_specs=[SMEM] + [VMEM] * 8,
        out_specs=(HBM, VMEM, VMEM, VMEM),
        input_output_aliases={4: 3},
        scratch_shapes=[
            pltpu.VMEM((16, BD, BD), BF),
            pltpu.VMEM((4, BD, BD), F32),
            pltpu.VMEM((4, BD, BD), F32),
            pltpu.SemaphoreType.DMA,
        ],
        compiler_params=params(14),
        name="corr_terms",
    )(
        src, wave, info, sums, work, other.reshape(2, 4, BD, BD), left, right_a, right_b,
    )

    pieces = lax.all_to_all(partial.reshape(128, 16, 128), ALL, 0, 0, tiled=True)
    copies = pl.pallas_call(
        sum_corr_kernel,
        out_shape=shape((32, 4, 16, 128)),
        in_specs=[VMEM, VMEM],
        out_specs=VMEM,
        compiler_params=params(8),
        name="sum_corr",
    )(info, pieces.reshape(32, 4, 16, 128))
    gathered = lax.all_to_all(copies, "op", 0, 0, tiled=True)
    applied_corr = pl.pallas_call(
        final_kernel,
        out_shape=shape((4, BD, BD), F32),
        in_specs=[VMEM, VMEM, VMEM],
        out_specs=HBM,
        scratch_shapes=[pltpu.VMEM((4, BD, BD), F32), pltpu.SemaphoreType.DMA((4,))],
        compiler_params=params(8),
        name="finish",
    )(info, gathered, corr)
    return (applied_wave, applied_corr)


def solution(mesh):
    placed = (
        P("blk", None, None),
        P("op", "blk", None, None),
        P("op", "blk", None, None),
        P("op", "blk"),
        P(None, "blk"),
        P("blk"),
    )
    return jax.shard_map(
        shards,
        mesh=mesh,
        in_specs=placed,
        out_specs=(P("blk", None, None), P("blk", None, None)),
        check_vma=False,
    )
```

```python
import jax
import jax.numpy as jnp
from jax import lax
from jax.experimental import pallas as pl
from jax.experimental.pallas import tpu as pltpu
from jax.sharding import PartitionSpec as P

BF = jnp.bfloat16
F32 = jnp.float32
BD = 256
INFO = 16
ROWS = BD + INFO
HALF = 8
STRIP = 32
MIB = 1 << 20
UNIT = 2.0 ** 20
SLOPE = 5.8
LN2 = 0.6931471805599453
ALL = ("op", "blk")

SMEM = pl.BlockSpec(memory_space=pltpu.SMEM)
VMEM = pl.BlockSpec(memory_space=pltpu.VMEM)
HBM = pl.BlockSpec(memory_space=pltpu.HBM)


def device(op, blk):
    return op * 4 + blk


def cross_pairs():
    return [(device(o, b), device(o ^ 16, b ^ 2)) for o in range(32) for b in range(4)]


def flip_pairs(bit):
    return [(o, o ^ bit) for o in range(32)]


def color_of(op):
    x, y, z = op & 1, (op >> 2) & 1, op >> 4
    return (x ^ z) + 2 * (y ^ z)


def core_pairs():
    return [(b, b ^ 1) for b in range(4)]


def core_groups():
    return [[device(o, zh * 2 + c) for zh in range(2) for o in range(32)] for c in range(2)]


def live(rows, cols, shape, first_row=0, first_col=0):
    row_ids = lax.broadcasted_iota(jnp.int32, shape, 0) + first_row
    col_ids = lax.broadcasted_iota(jnp.int32, shape, 1) + first_col
    return (row_ids < rows) & (col_ids < cols)


def pack(rows, cols, energy, wave):
    row = lax.broadcasted_iota(jnp.int32, (INFO, BD), 0)
    block = jnp.where(live(rows, cols, (BD, BD)), wave.astype(F32), 0.0)
    value = jnp.full((INFO, BD), energy, F32)
    high = value.astype(BF).astype(F32)
    middle = (value - high).astype(BF).astype(F32)
    low = value - high - middle
    info = jnp.zeros((INFO, BD), F32)
    for j, part in enumerate((rows.astype(F32), cols.astype(F32), high, middle, low)):
        info = jnp.where(row == j, part, info)
    return block.astype(BF), info.astype(BF)


def first_kernel(dims_in, energy_in, wave_in, out, dims, energy, wave, sems):
    b = color_of(lax.axis_index("op")) ^ 3
    copies = [
        pltpu.make_async_copy(dims_in, dims, sems.at[0]),
        pltpu.make_async_copy(energy_in, energy, sems.at[1]),
        pltpu.make_async_copy(wave_in.at[b], wave, sems.at[2]),
    ]
    for copy in copies:
        copy.start()
    for copy in copies:
        copy.wait()
    out[:BD], out[BD:] = pack(dims[0, b], dims[1, b], energy[b], wave[...])


def load_kernel(
    first, dims_in, energy_in, wave_in, left, right,
    own, left_out, right_out, token, dims, energy, wave, sems,
):
    copies = [
        pltpu.make_async_copy(dims_in, dims, sems.at[0]),
        pltpu.make_async_copy(energy_in, energy, sems.at[1]),
        pltpu.make_async_copy(wave_in, wave, sems.at[2]),
        pltpu.make_async_copy(left, left_out, sems.at[3]),
        pltpu.make_async_copy(right.at[pl.ds(0, HALF)], right_out, sems.at[4]),
    ]
    for copy in copies:
        copy.start()
    token[...] = jnp.zeros_like(token)
    for copy in copies[:3]:
        copy.wait()
    for b in range(4):
        own[b, :BD], own[b, BD:] = pack(dims[0, b], dims[1, b], energy[b], wave[b])
    for copy in copies[3:]:
        copy.wait()


def slot_terms(src, vec, left, right, e, first):
    inner = [
        jnp.dot(left[first + t, e], vec[src[e, first + t]], preferred_element_type=F32).astype(BF)
        for t in range(HALF)
    ]
    return lax.dot_general(
        jnp.concatenate(inner, axis=1),
        jnp.concatenate([right[t, e] for t in range(HALF)], axis=1),
        (((1,), (1,)), ((), ())),
        preferred_element_type=F32,
    )


def wave_kernel(
    src_in, own, core, far0, far1, far2, far3, near0, near1, near2, near3,
    left, right_a, right_in, token, out, vec, info, squares, right_b, src, acc, src_sem, sem,
):
    src_copy = pltpu.make_async_copy(src_in, src, src_sem)
    src_copy.start()
    right_copy = pltpu.make_async_copy(right_in.at[pl.ds(HALF, HALF)], right_b, sem)
    right_copy.start()
    me, color = lax.axis_index("blk"), color_of(lax.axis_index("op"))
    blocks = []
    for b in range(4):
        blocks.append((me * 4 + b, own.at[b]))
        blocks.append(((me ^ 1) * 4 + b, core.at[b]))
    for flip, pieces in ((2, (far0, far1, far2, far3)), (3, (near0, near1, near2, near3))):
        for b, piece in enumerate(pieces):
            blocks.append(((me ^ flip) * 4 + (color ^ b), piece))
    for block, piece in blocks:
        vec[block] = piece[:BD]
        entry = piece[BD:].astype(F32)
        info[block, 0:2] = entry[0:2]
        info[block, 2:3] = entry[2:3] + entry[3:4] + entry[4:5]
    src_copy.wait()
    plain, weighted = jnp.zeros((8, BD), F32), jnp.zeros((8, BD), F32)
    for e in range(4):
        acc[e] = slot_terms(src, vec, left, right_a, e, 0)
        for block in range(e * 4, e * 4 + 4):
            part = jnp.zeros((8, BD), F32)
            for r in range(0, BD, STRIP):
                vector = vec[block, r:r + STRIP].astype(F32)
                part += fold(vector * vector)
            plain += part
            weighted += info[block, 2:3] * part
    squares[0], squares[1] = plain, weighted
    right_copy.wait()
    for e in range(4):
        out[e] = encode(acc[e] + slot_terms(src, vec, left, right_b, e, HALF))


def encode(x):
    level = jnp.log(1.0 + jnp.abs(x) * UNIT) * (SLOPE / LN2)
    size = jnp.exp2(level - 120.0)
    return jnp.where(x < 0.0, -size, size).astype(BF)


def decode(code):
    code = code.astype(F32)
    size = jnp.abs(code)
    level = (jnp.log(size) * (1.0 / LN2) + 120.0) * (1.0 / SLOPE)
    value = jnp.where(size > 2.0 ** -120, (jnp.exp2(level) - 1.0) * (1.0 / UNIT), 0.0)
    return jnp.where(code < 0.0, -value, value)


def total_of(x):
    return jnp.sum(jnp.sum(x, axis=1, keepdims=True), axis=0, keepdims=True)


def fold(x):
    return jnp.sum(x.reshape(STRIP // 8, 8, BD), axis=0)


def decode_sums(work, codes, wave, me, turns, start):
    def add_group(group, cross):
        for turn in turns:
            b = me ^ turn
            for r in range(0, BD, STRIP):
                rows = pl.ds(r, STRIP)
                value = decode(codes[b >> 1, group, rows])
                work[group * 4 + b, rows] = value
                cross += fold(value * wave[group * 4 + b, rows].astype(F32))
        return cross

    return lax.fori_loop(0, 4, add_group, start)


def half_kernel(wave, squares, same, sums, work):
    sums[0] = squares[0]
    sums[1] = decode_sums(work, same, wave, lax.axis_index("blk"), (0, 2), squares[1])


def corr_kernel(
    src, wave, info, sums, work_in, other, left, right_a, right_b,
    applied_out, corr_out, out, work, vec, acc, applied, applied_sem,
):
    entries = 16 * BD * BD
    me = lax.axis_index("blk")
    zero = jnp.zeros((8, BD), F32)
    strips = [pl.ds(r, STRIP) for r in range(0, BD, STRIP)]

    square = sums[0]
    cross = decode_sums(work, other, wave, me, (1, 3), sums[1])
    rayleigh = total_of(cross) / entries / (total_of(square) / entries + 1e-06)

    def subtract(group, resid):
        for b in range(4):
            block = group * 4 + b
            level = info[block, 2:3] - rayleigh
            for rows in strips:
                rest = work[block, rows] + level * wave[block, rows].astype(F32)
                work[block, rows] = rest
                resid += fold(rest * rest)
        return resid

    resid = lax.fori_loop(0, 4, subtract, zero)
    scale = lax.rsqrt(total_of(resid) / entries + 1e-06)
    for b in range(4):
        for rows in strips:
            applied[b, rows] = work[me * 4 + b, rows] + rayleigh * wave[me * 4 + b, rows].astype(F32)

    applied_copy = pltpu.make_async_copy(applied, applied_out, applied_sem)
    applied_copy.start()

    @pl.loop(0, 4)
    def _(group):
        for b in range(4):
            for rows in strips:
                vec[group * 4 + b, rows] = (work[group * 4 + b, rows] * scale).astype(BF)

    for b in range(4):
        corr_out[b] = vec[me * 4 + b]

    for e in range(4):
        acc[e] = slot_terms(src, vec, left, right_a, e, 0)
    for e in range(4):
        total = acc[e] + slot_terms(src, vec, left, right_b, e, HALF)
        for i in range(16):
            for j in range(2):
                tile = total[i * 16:(i + 1) * 16, j * 128:(j + 1) * 128]
                out[i * 2 + j, e] = tile.astype(BF)
    applied_copy.wait()


def sum_wave_kernel(info, parts, out):
    part = lax.axis_index("op")
    entry = info[(part >> 3) * 4 + lax.axis_index("blk")]
    mask = live(entry[0:1], entry[1:2], (STRIP, BD), (part & 7) * STRIP)
    total = jnp.zeros((STRIP, BD), F32)
    for i in range(parts.shape[0]):
        total += decode(parts[i])
    total = encode(jnp.where(mask, total, 0.0))
    for i in range(out.shape[0]):
        out[i] = total


def sum_corr_kernel(info, parts, out):
    part = lax.axis_index("op")
    totals = []
    for b in range(4):
        entry = info[lax.axis_index("blk") * 4 + b][:, :128]
        total = jnp.sum(parts[:, b].astype(F32), axis=0)
        mask = live(entry[0:1], entry[1:2], (16, 128), (part >> 1) * 16, (part & 1) * 128)
        totals.append(jnp.where(mask, total, 0.0).astype(BF))
    for i in range(out.shape[0]):
        for b in range(4):
            out[i, b] = totals[b]


def final_kernel(info, parts, corr, out, blocks, sems):
    copies = []
    for b in range(4):
        level = info[lax.axis_index("blk") * 4 + b, 2:3]
        for i in range(16):
            rows = pl.ds(i * 16, 16)
            summed = jnp.concatenate([parts[2 * i, b], parts[2 * i + 1, b]], axis=1)
            blocks[b, rows] = summed.astype(F32) + level * corr[b, rows].astype(F32)
            if i % 8 == 7:
                done = pl.ds(i // 8 * 128, 128)
                place = sems.at[b * 2 + i // 8]
                copies.append(pltpu.make_async_copy(blocks.at[b, done], out.at[b, done], place))
                copies[-1].start()
    for copy in copies:
        copy.wait()


def params(mib):
    return pltpu.CompilerParams(vmem_limit_bytes=mib * MIB)


def shape(dims, kind=BF):
    return jax.ShapeDtypeStruct(dims, kind)


def shards(wave_blocks, left_env, right_env, source, block_dims, energy):
    src = source.T

    dims_in, energy_in, wave_in, left_in, right_in = (
        pltpu.with_memory_space_constraint(x, pltpu.HBM)
        for x in (block_dims, energy, wave_blocks, left_env, right_env)
    )
    half = (HALF,) + right_env.shape[1:]
    small = [pltpu.SMEM((2, 4), jnp.int32), pltpu.SMEM((4,), F32)]
    first = pl.pallas_call(
        first_kernel,
        out_shape=shape((ROWS, BD)),
        in_specs=[HBM] * 3,
        out_specs=VMEM,
        scratch_shapes=small + [pltpu.VMEM((BD, BD), BF), pltpu.SemaphoreType.DMA((3,))],
        compiler_params=params(2),
        name="pack_first",
    )(dims_in, energy_in, wave_in)
    far = [lax.ppermute(first, ALL, cross_pairs())]
    own, left, right_a, token = pl.pallas_call(
        load_kernel,
        out_shape=(
            shape((4, ROWS, BD)), pltpu.VMEM(left_env.shape, BF), pltpu.VMEM(half, BF),
            shape((8, 128), F32),
        ),
        in_specs=[VMEM] + [HBM] * 5,
        out_specs=(VMEM,) * 4,
        scratch_shapes=small + [pltpu.VMEM((4, BD, BD), BF), pltpu.SemaphoreType.DMA((5,))],
        compiler_params=params(4),
        name="load",
    )(first, dims_in, energy_in, wave_in, left_in, right_in)
    far[0], own, token = lax.optimization_barrier((far[0], own, token))
    core = lax.ppermute(own, "blk", core_pairs())
    for bit in (1, 4, 16):
        far.append(lax.ppermute(far[0], "op", flip_pairs(bit)))
    near = [lax.ppermute(piece, "blk", core_pairs()) for piece in far]

    partial, wave, info, squares, right_b = pl.pallas_call(
        wave_kernel,
        out_shape=(
            shape((4, BD, BD)), shape((16, BD, BD)), shape((16, 8, BD), F32),
            shape((2, 8, BD), F32), pltpu.VMEM(half, BF),
        ),
        in_specs=[HBM] + [VMEM] * 12 + [HBM, VMEM],
        out_specs=(VMEM,) * 5,
        scratch_shapes=[
            pltpu.SMEM((4, 16), jnp.int32),
            pltpu.VMEM((4, BD, BD), F32),
            pltpu.SemaphoreType.DMA,
            pltpu.SemaphoreType.DMA,
        ],
        compiler_params=params(8),
        name="wave_terms",
    )(
        pltpu.with_memory_space_constraint(src, pltpu.HBM), own, core, *far, *near,
        left, right_a, right_in, token,
    )

    pieces = lax.all_to_all(partial.reshape(32, 32, BD), "op", 0, 0, tiled=True)
    copies = pl.pallas_call(
        sum_wave_kernel,
        out_shape=shape((64, 32, BD)),
        in_specs=[VMEM, VMEM],
        out_specs=VMEM,
        compiler_params=params(8),
        name="sum_wave",
    )(info, pieces)
    same = lax.all_to_all(
        copies, ALL, 0, 0, tiled=True, axis_index_groups=core_groups()
    )
    other = lax.ppermute(same, "blk", core_pairs())
    sums, work = pl.pallas_call(
        half_kernel,
        out_shape=(shape((2, 8, BD), F32), shape((16, BD, BD), F32)),
        in_specs=[VMEM] * 3,
        out_specs=(VMEM, VMEM),
        compiler_params=params(2),
        cost_estimate=pl.CostEstimate(
            flops=16 * MIB, bytes_accessed=4 * MIB, transcendentals=MIB
        ),
        name="decode_half",
    )(wave, squares, same.reshape(2, 4, BD, BD))

    applied_wave, corr, partial, work = pl.pallas_call(
        corr_kernel,
        out_shape=(
            shape((4, BD, BD), F32), shape((4, BD, BD)), shape((32, 4, 16, 128)),
            shape((16, BD, BD), F32),
        ),
        in_specs=[SMEM] + [VMEM] * 8,
        out_specs=(HBM, VMEM, VMEM, VMEM),
        input_output_aliases={4: 3},
        scratch_shapes=[
            pltpu.VMEM((16, BD, BD), BF),
            pltpu.VMEM((4, BD, BD), F32),
            pltpu.VMEM((4, BD, BD), F32),
            pltpu.SemaphoreType.DMA,
        ],
        compiler_params=params(14),
        name="corr_terms",
    )(
        src, wave, info, sums, work, other.reshape(2, 4, BD, BD), left, right_a, right_b,
    )

    pieces = lax.all_to_all(partial.reshape(128, 16, 128), ALL, 0, 0, tiled=True)
    copies = pl.pallas_call(
        sum_corr_kernel,
        out_shape=shape((32, 4, 16, 128)),
        in_specs=[VMEM, VMEM],
        out_specs=VMEM,
        compiler_params=params(8),
        name="sum_corr",
    )(info, pieces.reshape(32, 4, 16, 128))
    gathered = lax.all_to_all(copies, "op", 0, 0, tiled=True)
    applied_corr = pl.pallas_call(
        final_kernel,
        out_shape=shape((4, BD, BD), F32),
        in_specs=[VMEM, VMEM, VMEM],
        out_specs=HBM,
        scratch_shapes=[pltpu.VMEM((4, BD, BD), F32), pltpu.SemaphoreType.DMA((8,))],
        compiler_params=params(8),
        name="finish",
    )(info, gathered, corr)
    return (applied_wave, applied_corr)


def solution(mesh):
    placed = (
        P("blk", None, None),
        P("op", "blk", None, None),
        P("op", "blk", None, None),
        P("op", "blk"),
        P(None, "blk"),
        P("blk"),
    )
    return jax.shard_map(
        shards,
        mesh=mesh,
        in_specs=placed,
        out_specs=(P("blk", None, None), P("blk", None, None)),
        check_vma=False,
    )
```
